128 devices in a mesh: grp: 8 (over x, core), row: 16 (over z, y).
Axes of the slice: x: 4, y: 4, z: 4, core: 2. Of those that a mesh axis runs over, the one named last changes fastest.
Arguments:
- lhs_emb: float32 [8, 4096, 400], P('grp', 'row'), may hold values from -3 to 3
- lhs_accum: float32 [8, 4096], P('grp', 'row'), may hold values from 0.5 to 20
- rhs_emb: float32 [8, 4096, 400], P('grp', 'row'), may hold values from -40 to 40
- rhs_accum: float32 [8, 4096], P('grp', 'row'), may hold values from 0.5 to 20
- rel_emb: float32 [1000, 400], replicated, may hold values from -3 to 3
- rel_accum: float32 [1000], replicated, may hold values from 5 to 500
- partner: int32 [8], P('grp'), may hold values from 0 to 7, as said below
- edge_lhs: int32 [8, 16, 2048], P('grp', 'row'), may hold values from 0 to 255
- edge_rhs: int32 [8, 16, 2048], P('grp', 'row'), may hold values from 0 to 4095, as said below
- edge_rel: int32 [8, 16, 2048], P('grp', 'row'), may hold values from 0 to 999
- edge_count: int32 [8, 16], P('grp', 'row'), may hold values from 1 to 2048, as said below
- neg_rhs: int32 [8, 16, 1024], P('grp', 'row'), may hold values from 0 to 4095, as said below
Outputs:
- new_lhs: float32 [8, 4096, 400], P('grp', 'row')
- new_lhs_accum: float32 [8, 4096], P('grp', 'row')
- new_rhs: float32 [8, 4096, 400], P('grp', 'row')
- new_rhs_accum: float32 [8, 4096], P('grp', 'row')
- new_rel: float32 [1000, 400], replicated
- new_rel_accum: float32 [1000], replicated
The draws below stay inside these ranges and needn't reach their ends.
Inputs may be any that keep to these rules, and one draw needn't show every extreme that they name: partner is a permutation of the groups; in it some group g trains the partition of group (g + 4) mod 8. `edge_count`: one device of every group has all 2048 slots live. `edge_rhs`: among the 2048 slots of each device, exactly 128 name a row of each block of 256 rows (rows k * 256 to (k + 1) * 256 - 1). `neg_rhs`: among the 1024 negatives of each device, exactly 64 name a row of each block of 256 rows.
All inputs are finite; a program needn't handle non-finite values.
Results may differ from the reference program's by a relative error of at most 0.003.
Values may be sent and summed in bfloat16 or wider, within the bound.
No kernel may reach another device: no remote copies, remote signals or barrier semaphores. Data moves between devices by JAX's collectives and lax.ppermute only.
A program may use at most 64 MiB of HBM per device.

```python
import math
import jax
import jax.numpy as jnp
import numpy as np
from jax import lax

D = 400
REL = 1000
NEG = 1024
R_DEV = 256
E_DEV = 2048
P_ROWS = 4096
N_GRP = 8
N_ROW = 16


def draw_rhs_emb(key, part):
    key = jax.random.fold_in(key, 11)
    first = jax.random.fold_in(key, 0)
    shape = (N_GRP, P_ROWS, D)
    return jnp.clip(0.5 * jax.random.normal(first, shape, jnp.float32), -3.0, 3.0)


def draw_partner(key, part):
    key = jax.random.fold_in(key, 5)
    first, second = jax.random.split(key)
    order = jax.random.permutation(first, N_GRP).astype(jnp.int32)
    chosen = jax.random.randint(second, (), 0, N_GRP).astype(jnp.int32)
    wanted = ((chosen + N_GRP // 2) % N_GRP).astype(jnp.int32)
    places = jnp.arange(N_GRP, dtype=jnp.int32)
    where_now = jnp.sum(jnp.where(order == wanted, places, 0)).astype(jnp.int32)
    held = order[chosen]
    order = order.at[where_now].set(held)
    order = order.at[chosen].set(wanted)
    return order.astype(jnp.int32)


def draw_edge_count(key, part):
    key = jax.random.fold_in(key, 7)
    first, second, third = jax.random.split(key, 3)
    shift = jax.random.randint(first, (N_GRP, N_ROW), 0, 4)
    jitter = jax.random.randint(second, (N_GRP, N_ROW), 0, max(E_DEV // 32, 1))
    counts = jnp.right_shift(jnp.full((N_GRP, N_ROW), E_DEV, jnp.int32), shift) - jitter
    fullest = jax.random.randint(third, (N_GRP, 1), 0, N_ROW)
    counts = jnp.where(jnp.arange(N_ROW, dtype=jnp.int32)[None, :] == fullest, E_DEV, counts)
    return jnp.maximum(counts, 1).astype(jnp.int32)


def balanced_rows(key, length):
    first, second = jax.random.split(key)
    blocks = jnp.tile(jnp.arange(N_ROW, dtype=jnp.int32), length // N_ROW)
    blocks = jnp.broadcast_to(blocks, (N_GRP, N_ROW, length))
    blocks = jax.random.permutation(first, blocks, axis=-1, independent=True)
    within = jax.random.randint(second, (N_GRP, N_ROW, length), 0, R_DEV)
    return (blocks * R_DEV + within).astype(jnp.int32)


def draw_edge_rhs(key, part):
    key = jax.random.fold_in(key, 13)
    return balanced_rows(key, E_DEV)


def draw_neg_rhs(key, part):
    key = jax.random.fold_in(key, 17)
    return balanced_rows(key, NEG)


def place_ends(result, stream_key, low, top_value):
    spot = [jax.random.randint(jax.random.fold_in(stream_key, axis), (), 0, length) for axis, length in enumerate(result.shape)]
    main_axis = result.shape.index(max(result.shape))
    beside = spot[:main_axis] + [(spot[main_axis] + 1) % result.shape[main_axis]] + spot[main_axis + 1:]
    return result.at[tuple(spot)].set(low).at[tuple(beside)].set(top_value)


def block_levels(stream_key, extent, shards, smallest, largest):
    level = 1.0
    for axis_at, shards_of in shards:
        steps = jax.random.uniform(jax.random.fold_in(jax.random.fold_in(stream_key, 6), axis_at), (shards_of,), jnp.float32, smallest / len(shards), largest / len(shards))
        level = level * jnp.repeat(jnp.exp(steps), extent[axis_at] // shards_of).reshape((-1,) + (1,) * (len(extent) - 1 - axis_at))
    return level


def rank_table(amount, slope):
    loads = [(1 << 20) // math.isqrt(rank ** slope) + 1 for rank in range(1, amount + 1)]
    width = 1 + sum(loads) // (1 << 30)
    return np.cumsum(np.array([max(1, weight // width) for weight in loads]))


def ranked_ids(key, shape, amount, lean):
    grid = rank_table(amount, lean)
    pick = jax.random.randint(jax.random.fold_in(key, 1), shape, 0, int(grid[amount - 1]))
    rank = jnp.searchsorted(jnp.asarray(grid, jnp.int32), pick, side="right")
    return jax.random.permutation(jax.random.fold_in(key, 2), amount)[rank].astype(jnp.int32)


def normal_values(stream_key, extent, deviation, limit, cuts=(), kind=jnp.bfloat16):
    gain = block_levels(stream_key, extent, cuts, -0.22, 0.18) if cuts else 1.0
    drawn = jax.random.normal(stream_key, extent, jnp.float32) * deviation * gain
    return jnp.minimum(jnp.maximum(drawn, -limit), limit).astype(kind)


def setup_inputs(seed: int = 0) -> dict:
    streams_of = jax.random.split(jax.random.key(seed), 13)
    return {
        "lhs_emb": normal_values(streams_of[0], (N_GRP, P_ROWS, D), 0.5, 3.0, ((0, 8), (1, 16)), jnp.float32),
        "lhs_accum": jnp.clip(jnp.exp(math.log(20.0) - 3.6888795 * jax.random.uniform(streams_of[1], (N_GRP, P_ROWS), jnp.float32) ** block_levels(streams_of[1], (N_GRP, P_ROWS), ((0, 8), (1, 16)), -0.2, 0.2)), 0.5, 20.0),
        "rhs_emb": draw_rhs_emb(jax.random.fold_in(streams_of[12], 71), 0),
        "rhs_accum": jnp.clip(jnp.exp(math.log(20.0) - 3.6888795 * jax.random.uniform(streams_of[3], (N_GRP, P_ROWS), jnp.float32) ** block_levels(streams_of[3], (N_GRP, P_ROWS), ((0, 8), (1, 16)), -0.2, 0.2)), 0.5, 20.0),
        "rel_emb": normal_values(streams_of[4], (REL, D), 0.5, 3.0, (), jnp.float32),
        "rel_accum": jnp.clip(jnp.exp(jax.random.uniform(streams_of[5], (REL,), jnp.float32, math.log(5.0), math.log(500.0))), 5.0, 500.0),
        "partner": draw_partner(jax.random.fold_in(streams_of[12], 71), 0),
        "edge_lhs": place_ends(jax.random.randint(streams_of[7], (N_GRP, N_ROW, E_DEV), 0, R_DEV), jax.random.fold_in(streams_of[7], 1), 0, R_DEV - 1).astype(jnp.int32),
        "edge_rhs": draw_edge_rhs(jax.random.fold_in(streams_of[12], 71), 0),
        "edge_rel": place_ends(ranked_ids(streams_of[9], (N_GRP, N_ROW, E_DEV), REL, 2), jax.random.fold_in(streams_of[9], 3), 0, REL - 1).astype(jnp.int32),
        "edge_count": draw_edge_count(jax.random.fold_in(streams_of[12], 71), 0),
        "neg_rhs": draw_neg_rhs(jax.random.fold_in(streams_of[12], 71), 0),
    }


LEARN = 0.25
TINY = 1e-10

def complex_mul(left, right):
    half = left.shape[-1] // 2
    left_a, left_b = (left[..., :half], left[..., half:])
    right_a, right_b = (right[..., :half], right[..., half:])
    return jnp.concatenate([left_a * right_a - left_b * right_b, left_a * right_b + left_b * right_a], -1)

def edge_terms(lhs_rows, rel_rows, pos_rows, neg_rows, live):
    query, pull = jax.vjp(complex_mul, lhs_rows, rel_rows)
    query_low = query.astype(jnp.bfloat16)
    pos_score = lax.optimization_barrier(jnp.sum(query_low.astype(jnp.float32) * pos_rows.astype(jnp.float32), -1))
    neg_score = lax.dot_general(query_low, neg_rows, (((1,), (1,)), ((), ())), preferred_element_type=jnp.float32)
    highest = jnp.maximum(pos_score, lax.optimization_barrier(jnp.max(neg_score, -1)))
    pos_exp = jnp.exp(pos_score - highest)
    neg_exp = jnp.exp(neg_score - highest[:, None])
    total = pos_exp + lax.optimization_barrier(jnp.sum(neg_exp, -1))
    pos_weight = live * (pos_exp / total - 1.0)
    neg_weight = (neg_exp * (live / total)[:, None]).astype(jnp.bfloat16)
    query_grad = pos_weight[:, None] * pos_rows.astype(jnp.float32) + jnp.dot(neg_weight, neg_rows, preferred_element_type=jnp.float32)
    lhs_grad, rel_grad = pull(query_grad)
    pos_grad = (pos_weight[:, None] * query_low.astype(jnp.float32)).astype(jnp.bfloat16)
    neg_grad = lax.dot_general(neg_weight, query_low, (((0,), (0,)), ((), ())), preferred_element_type=jnp.float32)
    return (lhs_grad, rel_grad, pos_grad, neg_grad)

def adagrad(table, accum, grad):
    new_accum = accum + lax.optimization_barrier(jnp.mean(grad * grad, -1))
    return (table - LEARN * grad / (jnp.sqrt(new_accum)[..., None] + TINY), new_accum)

def device_terms(lhs_table, right_low, lhs_index, rhs_index, rel_index, count, neg_index, rel_emb):
    live = (jnp.arange(E_DEV, dtype=jnp.int32) < count).astype(jnp.float32)
    lhs_grad, rel_grad, pos_grad, neg_grad = edge_terms(lhs_table[lhs_index], rel_emb[rel_index], right_low[rhs_index], right_low[neg_index], live)
    lhs_sum = jnp.zeros((R_DEV, D), jnp.float32).at[lhs_index].add(lhs_grad)
    rel_sum = jnp.zeros((REL, D), jnp.float32).at[rel_index].add(rel_grad)
    return (lhs_sum, rel_sum, pos_grad, neg_grad.astype(jnp.bfloat16))

def reference(lhs_emb, lhs_accum, rhs_emb, rhs_accum, rel_emb, rel_accum, partner, edge_lhs, edge_rhs, edge_rel, edge_count, neg_rhs):

    def one_group(group):
        source = partner[group]
        rhs_table = rhs_emb[source]
        right_low = rhs_table.astype(jnp.bfloat16)
        lhs_tables = lhs_emb[group].reshape(N_ROW, R_DEV, D)

        def one_device(device):
            return device_terms(lhs_tables[device], right_low, edge_lhs[group, device], edge_rhs[group, device], edge_rel[group, device], edge_count[group, device], neg_rhs[group, device], rel_emb)
        lhs_sums, rel_sums, pos_grads, neg_grads = lax.map(one_device, jnp.arange(N_ROW, dtype=jnp.int32))
        rhs_grad = jnp.zeros((P_ROWS, D), jnp.float32)
        rhs_grad = rhs_grad.at[edge_rhs[group].reshape(-1)].add(pos_grads.reshape(-1, D).astype(jnp.float32))
        rhs_grad = rhs_grad.at[neg_rhs[group].reshape(-1)].add(neg_grads.reshape(-1, D).astype(jnp.float32))
        new_lhs, new_lhs_accum = adagrad(lhs_emb[group], lhs_accum[group], lhs_sums.reshape(P_ROWS, D))
        new_rhs, new_rhs_accum = adagrad(rhs_table, rhs_accum[source], rhs_grad)
        return (new_lhs, new_lhs_accum, new_rhs, new_rhs_accum, lax.optimization_barrier(jnp.sum(rel_sums, 0)))
    results = lax.map(one_group, jnp.arange(N_GRP, dtype=jnp.int32))
    rel_grad = lax.optimization_barrier(jnp.sum(results[4], 0))
    new_rel, new_rel_accum = adagrad(rel_emb, rel_accum, rel_grad)
    return (results[0], results[1], results[2], results[3], new_rel, new_rel_accum)
```

```python
import functools

import jax
import jax.numpy as jnp
from jax import lax
from jax.experimental import pallas as pl
from jax.experimental.pallas import tpu as pltpu
from jax.sharding import PartitionSpec as P

LEARN = 0.25
TINY = 1e-10
BF = jnp.bfloat16
F32 = jnp.float32
D = 400
HALF = 200
REL = 1000
RELP = 1024
LOCAL = 256
EDGES = 2048
NEG = 1024
OWNERS = 16
PER = 128
FOLD = 208
SEND = D + FOLD
CHUNK = 256
STEPS = EDGES // CHUNK
VMEM = 50 * 1024 * 1024


def onehot(index, count):
    rows = lax.broadcasted_iota(jnp.int32, (count, index.shape[1]), 0)
    return jnp.where(rows == index, 1.0, 0.0).astype(BF)


def dot(a, b):
    return jnp.dot(a, b, preferred_element_type=F32)


def dot_t(a, b):
    return lax.dot_general(a, b, (((1,), (1,)), ((), ())), preferred_element_type=F32)


def split(value):
    high = value.astype(BF)
    return high, (value - high.astype(F32)).astype(BF)


def lhs_of(packed):
    return jnp.bitwise_and(jnp.right_shift(packed, 1), LOCAL - 1)


def rel_of(packed):
    return jnp.bitwise_and(jnp.right_shift(packed, 9), RELP - 1)


def query_kernel(packed_ref, lhs_ref, rel_ref, l_ref, w_ref, q_ref, lhs_two, rel_two):
    @pl.when(pl.program_id(0) == 0)
    def _():
        high, low = split(lhs_ref[...])
        lhs_two[0:D, :] = high
        lhs_two[D : 2 * D, :] = low
        rel_two[...] = jnp.zeros_like(rel_two)
        high, low = split(rel_ref[...])
        rel_two[0:D, 0:REL] = high
        rel_two[D : 2 * D, 0:REL] = low

    packed = packed_ref[...]
    both = dot(lhs_two[...], onehot(lhs_of(packed), LOCAL))
    left = both[0:D] + both[D : 2 * D]
    both = dot(rel_two[...], onehot(rel_of(packed), RELP))
    weight = both[0:D] + both[D : 2 * D]
    l_ref[...] = left
    w_ref[...] = weight
    la, lb, wa, wb = left[:HALF], left[HALF:], weight[:HALF], weight[HALF:]
    q_ref[...] = jnp.concatenate([la * wa - lb * wb, la * wb + lb * wa], 0).astype(BF)


def make_query(packed, lhs_t, rel_t):
    wide = pl.BlockSpec((D, CHUNK), lambda i: (0, i))
    return pl.pallas_call(
        query_kernel,
        grid=(STEPS,),
        in_specs=[
            pl.BlockSpec((1, CHUNK), lambda i: (0, i)),
            pl.BlockSpec((D, LOCAL), lambda i: (0, 0)),
            pl.BlockSpec((D, REL), lambda i: (0, 0)),
        ],
        out_specs=[wide, wide, wide],
        out_shape=[
            jax.ShapeDtypeStruct((D, EDGES), F32),
            jax.ShapeDtypeStruct((D, EDGES), F32),
            jax.ShapeDtypeStruct((D, EDGES), BF),
        ],
        scratch_shapes=[pltpu.VMEM((2 * D, LOCAL), BF), pltpu.VMEM((2 * D, RELP), BF)],
        compiler_params=pltpu.CompilerParams(vmem_limit_bytes=VMEM),
        cost_estimate=pl.CostEstimate(flops=5_000_000_000, bytes_accessed=10_000_000, transcendentals=0),
        name="make_query",
    )(packed, lhs_t, rel_t)


def fold_marks(index):
    marks = onehot(index, LOCAL)
    first = lax.broadcasted_iota(jnp.int32, marks.shape, 1) < 64
    none = jnp.zeros_like(marks)
    return jnp.where(first, marks, none), jnp.where(first, none, marks)


def serve_kernel(partner_ref, table_ref, asked_ref, rhs_ref, accum_ref, out_ref, ext_ref, two):
    del partner_ref
    table = table_ref[0]
    two[:, 0:LOCAL] = table[0:FOLD]
    two[0 : D - FOLD, LOCAL : 2 * LOCAL] = table[FOLD:D]
    two[D - FOLD : FOLD, LOCAL : 2 * LOCAL] = jnp.zeros((2 * FOLD - D, LOCAL), BF)
    for s in range(0, OWNERS, 2):
        pos = jnp.concatenate([asked_ref[s, 0:1, :], asked_ref[s + 1, 0:1, :]], 1)
        rows = dot(table, onehot(pos, LOCAL)).astype(BF)
        out_ref[s, 0:D, :] = rows[:, 0:PER]
        out_ref[s + 1, 0:D, :] = rows[:, PER:]
        marks = [jnp.concatenate(fold_marks(asked_ref[t, 1:2, :]), 0) for t in (s, s + 1)]
        rows = dot(two[...], jnp.concatenate(marks, 1)).astype(BF)
        out_ref[s, D:SEND, :] = rows[:, 0:PER]
        out_ref[s + 1, D:SEND, :] = rows[:, PER:]
    ext_ref[0:D, :] = rhs_ref[...]
    ext_ref[D : D + 8, :] = jnp.broadcast_to(accum_ref[...], (8, LOCAL))


def serve(partner, tables, asked, rhs_t, accum):
    whole = lambda shape: pl.BlockSpec(shape, lambda i, p: (0,) * len(shape))
    return pl.pallas_call(
        serve_kernel,
        grid_spec=pltpu.PrefetchScalarGridSpec(
            num_scalar_prefetch=1,
            grid=(1,),
            in_specs=[
                pl.BlockSpec((1, D, LOCAL), lambda i, p: (p[0], 0, 0)),
                whole((OWNERS, 8, PER)),
                whole((D, LOCAL)),
                whole((1, LOCAL)),
            ],
            out_specs=[whole((OWNERS, SEND, PER)), whole((D + 8, LOCAL))],
            scratch_shapes=[pltpu.VMEM((FOLD, 2 * LOCAL), BF)],
        ),
        out_shape=[
            jax.ShapeDtypeStruct((OWNERS, SEND, PER), BF),
            jax.ShapeDtypeStruct((D + 8, LOCAL), F32),
        ],
        compiler_params=pltpu.CompilerParams(vmem_limit_bytes=VMEM),
        cost_estimate=pl.CostEstimate(flops=2_000_000_000, bytes_accessed=5_000_000, transcendentals=0),
        name="serve_rows",
    )(partner, tables, asked, rhs_t, accum)


def edge_kernel(packed_ref, got_ref, q_ref, l_ref, w_ref, back_ref, rel_ref, lhs_ref, neg_t, neg_n, weights, lhs_g, lhs_lo, rel_g, q_all, m_lhs, m_rel):
    step = pl.program_id(0)

    @pl.when(step == 0)
    def _():
        for k in range(0, OWNERS, 2):
            a, b = got_ref[k, D:SEND, :].astype(F32), got_ref[k + 1, D:SEND, :].astype(F32)
            first = lax.broadcasted_iota(jnp.int32, a.shape, 1) < 64
            top = jnp.where(first, a, pltpu.roll(b, 64, 1))
            low = jnp.where(first, pltpu.roll(a, 64, 1), b)
            both = jnp.concatenate([top, low[0 : D - FOLD]], 0)
            lanes = slice(k * 64, k * 64 + PER)
            neg_t[:, lanes] = both.astype(BF)
            neg_n[lanes, :] = both.T.astype(BF)

    lanes = pl.ds(pl.multiple_of(step * CHUNK, CHUNK), CHUNK)
    packed = packed_ref[...]
    live = jnp.bitwise_and(packed, 1).astype(F32)
    query = q_ref[...]
    query_wide = query.astype(F32)
    pos = jnp.concatenate([got_ref[2 * step, 0:D, :], got_ref[2 * step + 1, 0:D, :]], 1).astype(F32)
    scores = dot(neg_n[...], query)
    pos_score = jnp.sum(query_wide * pos, 0, keepdims=True)
    highest = jnp.maximum(pos_score, jnp.max(scores, 0, keepdims=True))
    neg_exp = jnp.exp(scores - highest)
    pos_exp = jnp.exp(pos_score - highest)
    total = pos_exp + jnp.sum(neg_exp, 0, keepdims=True)
    pos_weight = live * (pos_exp / total - 1.0)
    weight = (neg_exp * (live / total)).astype(BF)
    weights[:, lanes] = weight
    grad = pos_weight * pos + dot(neg_t[...], weight)
    pos_grad = (pos_weight * query_wide).astype(BF)
    back_ref[2 * step, 0:D, :] = pos_grad[:, 0:PER]
    back_ref[2 * step + 1, 0:D, :] = pos_grad[:, PER:]
    ga, gb = grad[:HALF], grad[HALF:]
    left, rel = l_ref[...], w_ref[...]
    la, lb, wa, wb = left[:HALF], left[HALF:], rel[:HALF], rel[HALF:]
    high, low = split(jnp.concatenate([ga * wa + gb * wb, gb * wa - ga * wb], 0))
    lhs_g[:, lanes] = high
    lhs_lo[:, lanes] = low
    rel_g[:, lanes] = jnp.concatenate([ga * la + gb * lb, gb * la - ga * lb], 0).astype(BF)
    q_all[:, lanes] = query
    m_lhs[:, lanes] = onehot(lhs_of(packed), LOCAL)
    m_rel[:, lanes] = onehot(rel_of(packed), RELP)

    @pl.when(step == STEPS - 1)
    def _():
        for t in range(0, RELP // PER, 2):
            part = dot_t(rel_g[...], m_rel[t * PER : (t + 2) * PER, :]).astype(BF)
            rel_ref[t, 0:D, :] = part[:, 0:PER]
            rel_ref[t + 1, 0:D, :] = part[:, PER:]
            rel_ref[t, D:512, :] = jnp.zeros((112, PER), BF)
            rel_ref[t + 1, D:512, :] = jnp.zeros((112, PER), BF)
        for k in range(0, OWNERS, 4):
            part = dot_t(q_all[...], weights[k * 64 : (k + 4) * 64, :])
            for h in (0, 2):
                both = part[:, h * 64 : (h + 2) * 64]
                top = both[0:FOLD]
                low = jnp.concatenate([both[FOLD:D], jnp.zeros((2 * FOLD - D, PER), F32)], 0)
                first = lax.broadcasted_iota(jnp.int32, top.shape, 1) < 64
                back_ref[k + h, D:SEND, :] = jnp.where(first, top, pltpu.roll(low, 64, 1)).astype(BF)
                back_ref[k + h + 1, D:SEND, :] = jnp.where(first, pltpu.roll(top, 64, 1), low).astype(BF)
        lhs_ref[...] = dot_t(lhs_g[...], m_lhs[...]) + dot_t(lhs_lo[...], m_lhs[...])


def edges(packed, got, query, left, weight):
    wide = pl.BlockSpec((D, CHUNK), lambda i: (0, i))
    whole = lambda shape: pl.BlockSpec(shape, lambda i: (0,) * len(shape))
    return pl.pallas_call(
        edge_kernel,
        grid=(STEPS,),
        in_specs=[
            pl.BlockSpec((1, CHUNK), lambda i: (0, i)),
            whole((OWNERS, SEND, PER)),
            wide,
            wide,
            wide,
        ],
        out_specs=[whole((OWNERS, SEND, PER)), whole((RELP // PER, 512, PER)), whole((D, LOCAL))],
        out_shape=[
            jax.ShapeDtypeStruct((OWNERS, SEND, PER), BF),
            jax.ShapeDtypeStruct((RELP // PER, 512, PER), BF),
            jax.ShapeDtypeStruct((D, LOCAL), F32),
        ],
        scratch_shapes=[
            pltpu.VMEM((D, NEG), BF),
            pltpu.VMEM((NEG, D), BF),
            pltpu.VMEM((NEG, EDGES), BF),
            pltpu.VMEM((D, EDGES), BF),
            pltpu.VMEM((D, EDGES), BF),
            pltpu.VMEM((D, EDGES), BF),
            pltpu.VMEM((D, EDGES), BF),
            pltpu.VMEM((LOCAL, EDGES), BF),
            pltpu.VMEM((RELP, EDGES), BF),
        ],
        compiler_params=pltpu.CompilerParams(vmem_limit_bytes=VMEM),
        cost_estimate=pl.CostEstimate(flops=10_000_000_000, bytes_accessed=20_000_000, transcendentals=2_100_000),
        name="edges",
    )(packed, got, query, left, weight)


def adagrad(table, accum, grad):
    new_accum = accum + jnp.mean(grad * grad, 0, keepdims=True)
    return table - LEARN * grad / (jnp.sqrt(new_accum) + TINY), new_accum


def right_kernel(partner_ref, ext_ref, asked_ref, back_ref, new_ref, accum_ref, pos, neg, m_pos, m_one, m_two):
    del partner_ref
    for s in range(OWNERS):
        lanes = slice(s * PER, (s + 1) * PER)
        pos[:, lanes] = back_ref[s, 0:D, :]
        neg[:, lanes] = back_ref[s, D:SEND, :]
        m_pos[:, lanes] = onehot(asked_ref[s, 0:1, :], LOCAL)
        one, two = fold_marks(asked_ref[s, 1:2, :])
        m_one[:, lanes] = one
        m_two[:, lanes] = two
    low = dot_t(neg[...], m_two[...])[0 : D - FOLD]
    grad = dot_t(pos[...], m_pos[...]) + jnp.concatenate([dot_t(neg[...], m_one[...]), low], 0)
    new_ref[...], accum_ref[...] = adagrad(ext_ref[0, 0:D, :], ext_ref[0, D : D + 1, :], grad)


def right_update(partner, ext_all, asked, back):
    whole = lambda shape: pl.BlockSpec(shape, lambda i, p: (0,) * len(shape))
    marks = pltpu.VMEM((LOCAL, OWNERS * PER), BF)
    return pl.pallas_call(
        right_kernel,
        grid_spec=pltpu.PrefetchScalarGridSpec(
            num_scalar_prefetch=1,
            grid=(1,),
            in_specs=[
                pl.BlockSpec((1, D + 8, LOCAL), lambda i, p: (p[0], 0, 0)),
                whole((OWNERS, 8, PER)),
                whole((OWNERS, SEND, PER)),
            ],
            out_specs=[whole((D, LOCAL)), whole((1, LOCAL))],
            scratch_shapes=[
                pltpu.VMEM((D, OWNERS * PER), BF),
                pltpu.VMEM((FOLD, OWNERS * PER), BF),
                marks,
                marks,
                marks,
            ],
        ),
        out_shape=[jax.ShapeDtypeStruct((D, LOCAL), F32), jax.ShapeDtypeStruct((1, LOCAL), F32)],
        compiler_params=pltpu.CompilerParams(vmem_limit_bytes=VMEM),
        cost_estimate=pl.CostEstimate(flops=2_000_000_000, bytes_accessed=5_000_000, transcendentals=0),
        name="right_update",
    )(partner, ext_all, asked, back)


def left_kernel(table_ref, accum_ref, grad_ref, new_ref, new_accum_ref):
    new_ref[...], new_accum_ref[...] = adagrad(table_ref[...], accum_ref[...], grad_ref[...])


def left_update(table, accum, grad):
    return pl.pallas_call(
        left_kernel,
        out_shape=[jax.ShapeDtypeStruct((D, LOCAL), F32), jax.ShapeDtypeStruct((1, LOCAL), F32)],
        name="left_update",
    )(table, accum, grad)


def relation_kernel(table_ref, accum_ref, grad_ref, new_ref, new_accum_ref):
    grad = grad_ref[0, 0:D, :].astype(F32)
    new_ref[...], new_accum_ref[...] = adagrad(table_ref[...], accum_ref[...], grad)


def relation_update(table, accum, grad):
    tall = pl.BlockSpec((D, PER), lambda i: (0, i))
    flat = pl.BlockSpec((1, PER), lambda i: (0, i))
    return pl.pallas_call(
        relation_kernel,
        grid=(RELP // PER,),
        in_specs=[tall, flat, pl.BlockSpec((1, 512, PER), lambda i: (i, 0, 0))],
        out_specs=[tall, flat],
        out_shape=[jax.ShapeDtypeStruct((D, REL), F32), jax.ShapeDtypeStruct((1, REL), F32)],
        name="relation_update",
    )(table, accum, grad)


def body(
    lhs_emb,
    lhs_accum,
    rhs_emb,
    rhs_accum,
    rel_emb,
    rel_accum,
    partner,
    edge_lhs,
    edge_rhs,
    edge_rel,
    edge_count,
    neg_rhs,
):
    lhs_t, rhs_t, rel_t = lhs_emb[0].T, rhs_emb[0].T, rel_emb.T
    tables = lax.all_gather(rhs_t.astype(BF), "grp", axis=0, tiled=False)

    live = (jnp.arange(EDGES, dtype=jnp.int32) < edge_count[0, 0]).astype(jnp.int32)
    packed = lax.sort(
        (edge_rhs[0, 0] << 19) | (edge_rel[0, 0] << 9) | (edge_lhs[0, 0] << 1) | live, is_stable=False
    )
    neg_index = lax.sort(neg_rhs[0, 0], is_stable=False)
    pos_ask = ((packed >> 19) & (LOCAL - 1)).reshape(OWNERS, 1, PER)
    neg_ask = (neg_index & (LOCAL - 1)).reshape(OWNERS, 1, 64)
    ask = jnp.concatenate(
        [pos_ask, jnp.concatenate([neg_ask, neg_ask], 2), jnp.zeros((OWNERS, 6, PER), jnp.int32)], 1
    )
    asked = lax.all_to_all(ask, "row", 0, 0, tiled=True)
    packed = packed.reshape(1, EDGES)
    left, weight, query = make_query(packed, lhs_t, rel_t)

    rows, ext = serve(partner, tables, asked, rhs_t, rhs_accum)
    ext_all = lax.all_gather(ext, "grp", axis=0, tiled=False)
    got = lax.all_to_all(rows, "row", 0, 0, tiled=True)
    back, rel_sum, lhs_sum = edges(packed, got, query, left, weight)

    parts = lax.all_to_all(rel_sum.reshape(128, 32, PER), ("grp", "row"), 0, 0, tiled=True)
    returned = lax.all_to_all(back, "row", 0, 0, tiled=True)
    shard = jnp.sum(parts.astype(F32), 0).astype(BF)
    rel_grad = lax.all_to_all(jnp.broadcast_to(shard[None], (128, 32, PER)), ("grp", "row"), 0, 0, tiled=True)

    new_lhs, new_lhs_accum = left_update(lhs_t, lhs_accum, lhs_sum)
    new_rhs, new_rhs_accum = right_update(partner, ext_all, asked, returned)
    new_rel, new_rel_accum = relation_update(rel_t, rel_accum[None], rel_grad.reshape(RELP // PER, 512, PER))
    return (
        new_lhs.T[None],
        new_lhs_accum,
        new_rhs.T[None],
        new_rhs_accum,
        new_rel.T,
        new_rel_accum[0],
    )


def solution(mesh):
    rows = P("grp", "row", None)
    in_specs = (
        rows,
        P("grp", "row"),
        rows,
        P("grp", "row"),
        P(),
        P(),
        P("grp"),
        rows,
        rows,
        rows,
        P("grp", "row"),
        rows,
    )
    out_specs = (rows, P("grp", "row"), rows, P("grp", "row"), P(), P())
    return jax.shard_map(body, mesh=mesh, in_specs=in_specs, out_specs=out_specs, check_vma=False)
```

```python
import jax
import jax.numpy as jnp
from jax import lax
from jax.experimental import pallas as pl
from jax.experimental.pallas import tpu as pltpu
from jax.sharding import PartitionSpec as P

LEARN = 0.25
TINY = 1e-10
BF = jnp.bfloat16
F32 = jnp.float32
D = 400
HALF = 200
REL = 1000
RELP = 1024
LOCAL = 256
EDGES = 2048
NEG = 1024
OWNERS = 16
PER = 128
FOLD = 208
SEND = D + FOLD
BACK = SEND + 16
CHUNK = 256
STEPS = EDGES // CHUNK
SUB = 2
MIB = 1024 * 1024


def onehot(index, count):
    rows = lax.broadcasted_iota(jnp.int32, (count, index.shape[1]), 0)
    return jnp.where(rows == index, 1.0, 0.0).astype(BF)


def dot(a, b):
    return jnp.dot(a, b, preferred_element_type=F32)


def dot_t(a, b):
    return lax.dot_general(a, b, (((1,), (1,)), ((), ())), preferred_element_type=F32)


def split(value):
    high = value.astype(BF)
    return high, (value - high.astype(F32)).astype(BF)


def lhs_of(packed):
    return jnp.bitwise_and(jnp.right_shift(packed, 1), LOCAL - 1)


def rel_of(packed):
    return jnp.bitwise_and(jnp.right_shift(packed, 9), RELP - 1)


def query_kernel(packed_ref, lhs_ref, rel_ref, l_ref, w_ref, q_ref, lhs_two, rel_two):
    @pl.when(pl.program_id(0) == 0)
    def _():
        high, low = split(lhs_ref[...])
        lhs_two[0:D, :] = high
        lhs_two[D : 2 * D, :] = low
        rel_two[...] = jnp.zeros_like(rel_two)
        high, low = split(rel_ref[...])
        rel_two[0:D, 0:REL] = high
        rel_two[D : 2 * D, 0:REL] = low

    packed = packed_ref[...]
    both = dot(lhs_two[...], onehot(lhs_of(packed), LOCAL))
    left = both[0:D] + both[D : 2 * D]
    both = dot(rel_two[...], onehot(rel_of(packed), RELP))
    weight = both[0:D] + both[D : 2 * D]
    l_ref[...] = left
    w_ref[...] = weight
    la, lb, wa, wb = left[:HALF], left[HALF:], weight[:HALF], weight[HALF:]
    q_ref[...] = jnp.concatenate([la * wa - lb * wb, la * wb + lb * wa], 0).astype(BF)


def make_query(packed, lhs_t, rel_t):
    wide = pl.BlockSpec((D, CHUNK), lambda i: (0, i))
    return pl.pallas_call(
        query_kernel,
        grid=(STEPS,),
        in_specs=[
            pl.BlockSpec((1, CHUNK), lambda i: (0, i)),
            pl.BlockSpec((D, LOCAL), lambda i: (0, 0)),
            pl.BlockSpec((D, REL), lambda i: (0, 0)),
        ],
        out_specs=[wide, wide, wide],
        out_shape=[
            jax.ShapeDtypeStruct((D, EDGES), F32),
            jax.ShapeDtypeStruct((D, EDGES), F32),
            jax.ShapeDtypeStruct((D, EDGES), BF),
        ],
        scratch_shapes=[pltpu.VMEM((2 * D, LOCAL), BF), pltpu.VMEM((2 * D, RELP), BF)],
        compiler_params=pltpu.CompilerParams(vmem_limit_bytes=58 * MIB),
        cost_estimate=pl.CostEstimate(flops=5_000_000_000, bytes_accessed=10_000_000, transcendentals=0),
        name="make_query",
    )(packed, lhs_t, rel_t)


def fold_marks(marks):
    first = lax.broadcasted_iota(jnp.int32, marks.shape, 1) < 64
    none = jnp.zeros_like(marks)
    return jnp.where(first, marks, none), jnp.where(first, none, marks)


def twice(row):
    first = lax.broadcasted_iota(jnp.int32, row.shape, 1) < 64
    turned = pltpu.roll(row, 64, 1)
    return jnp.where(first, row, turned), jnp.where(first, turned, row)


def labels(pos, neg):
    row = lax.broadcasted_iota(jnp.int32, (16, PER), 0)
    return jnp.where(row == 0, pos, jnp.where(row == 1, neg, 0)).astype(F32).astype(BF)


def edge_kernel(
    place_ref, packed_ref, neg_ref, a0, a1, a2, a3, b0, b1, b2, b3, q_ref, l_ref, w_ref,
    back_ref, lhs_g, lhs_lo, rel_g, table, neg_t, neg_n, weights, q_all,
):
    step = pl.program_id(0)

    @pl.when(step == 0)
    def _():
        for z, a in enumerate((a0, a1, a2, a3)):
            for y, b in enumerate((b0, b1, b2, b3)):
                table[4 * z + y, :, 0:PER] = a[y]
                table[4 * z + y, :, PER:LOCAL] = b[z]
        for c in range(STEPS):
            here = jnp.bitwise_and(neg_ref[c : c + 1, :], LOCAL - 1)
            one, two = fold_marks(onehot(here, LOCAL))
            rows = dot(table[2 * c], one) + dot(table[2 * c + 1], two)
            lanes = slice(c * PER, (c + 1) * PER)
            neg_t[:, lanes] = rows.astype(BF)
            neg_n[lanes, :] = rows.T.astype(BF)

    for h in range(SUB):
        part = step * SUB + h
        lanes = pl.ds(pl.multiple_of(part * CHUNK, CHUNK), CHUNK)
        own = slice(h * CHUNK, (h + 1) * CHUNK)
        packed = packed_ref[:, own]
        live = jnp.bitwise_and(packed, 1).astype(F32)
        query = q_ref[:, own]
        query_wide = query.astype(F32)
        asked = jnp.bitwise_and(jnp.right_shift(packed, 19), LOCAL - 1)
        marks = onehot(asked, LOCAL)
        pos = jnp.concatenate([dot(table[2 * part], marks[:, 0:PER]), dot(table[2 * part + 1], marks[:, PER:])], 1)
        scores = dot(neg_n[...], query)
        pos_score = jnp.sum(query_wide * pos, 0, keepdims=True)
        highest = jnp.maximum(pos_score, jnp.max(scores, 0, keepdims=True))
        neg_exp = jnp.exp(scores - highest)
        pos_exp = jnp.exp(pos_score - highest)
        total = pos_exp + jnp.sum(neg_exp, 0, keepdims=True)
        pos_weight = live * (pos_exp / total - 1.0)
        weight = (neg_exp * (live / total)).astype(BF)
        weights[:, lanes] = weight
        grad = pos_weight * pos + dot(neg_t[...], weight)
        pos_grad = (pos_weight * query_wide).astype(BF)
        one, two = twice(jnp.bitwise_and(neg_ref[pl.ds(part, 1), :], LOCAL - 1))
        k, m = place_ref[2 * part], place_ref[2 * part + 1]
        back_ref[k, 0:D, :] = pos_grad[:, 0:PER]
        back_ref[m, 0:D, :] = pos_grad[:, PER:]
        back_ref[k, SEND:BACK, :] = labels(asked[:, 0:PER], one)
        back_ref[m, SEND:BACK, :] = labels(asked[:, PER:], two)
        ga, gb = grad[:HALF], grad[HALF:]
        left, rel = l_ref[:, own], w_ref[:, own]
        la, lb, wa, wb = left[:HALF], left[HALF:], rel[:HALF], rel[HALF:]
        lhs_g[:, own], lhs_lo[:, own] = split(jnp.concatenate([ga * wa + gb * wb, gb * wa - ga * wb], 0))
        rel_g[:, own] = jnp.concatenate([ga * la + gb * lb, gb * la - ga * lb], 0).astype(BF)
        q_all[:, lanes] = query

    @pl.when(step == STEPS // SUB - 1)
    def _():
        for c in range(0, STEPS, 2):
            part = dot_t(q_all[...], weights[c * PER : (c + 2) * PER, :])
            for h in (0, 1):
                both = part[:, h * PER : (h + 1) * PER]
                top = both[0:FOLD]
                low = jnp.concatenate([both[FOLD:D], jnp.zeros((2 * FOLD - D, PER), F32)], 0)
                first = lax.broadcasted_iota(jnp.int32, top.shape, 1) < 64
                at = 2 * (c + h)
                back_ref[place_ref[at], D:SEND, :] = jnp.where(first, top, pltpu.roll(low, 64, 1)).astype(BF)
                back_ref[place_ref[at + 1], D:SEND, :] = jnp.where(first, pltpu.roll(top, 64, 1), low).astype(BF)


def edges(place, packed, neg, halves, query, left, weight):
    wide = pl.BlockSpec((D, SUB * CHUNK), lambda i, p: (0, i))
    whole = lambda shape: pl.BlockSpec(shape, lambda i, p: (0,) * len(shape))
    return pl.pallas_call(
        edge_kernel,
        grid_spec=pltpu.PrefetchScalarGridSpec(
            num_scalar_prefetch=1,
            grid=(STEPS // SUB,),
            in_specs=[pl.BlockSpec((1, SUB * CHUNK), lambda i, p: (0, i)), whole((STEPS, PER))]
            + [whole((4, D, PER))] * 8
            + [wide, wide, wide],
            out_specs=[whole((OWNERS, BACK, PER)), wide, wide, wide],
            scratch_shapes=[
                pltpu.VMEM((OWNERS, D, LOCAL), BF),
                pltpu.VMEM((D, NEG), BF),
                pltpu.VMEM((NEG, D), BF),
                pltpu.VMEM((NEG, EDGES), BF),
                pltpu.VMEM((D, EDGES), BF),
            ],
        ),
        out_shape=[
            jax.ShapeDtypeStruct((OWNERS, BACK, PER), BF),
            jax.ShapeDtypeStruct((D, EDGES), BF),
            jax.ShapeDtypeStruct((D, EDGES), BF),
            jax.ShapeDtypeStruct((D, EDGES), BF),
        ],
        compiler_params=pltpu.CompilerParams(vmem_limit_bytes=58 * MIB),
        cost_estimate=pl.CostEstimate(flops=8_000_000_000, bytes_accessed=20_000_000, transcendentals=2_100_000),
        name="edges",
    )(place, packed, neg, *halves, query, left, weight)


def sums_kernel(core_ref, packed_ref, lhs_g, lhs_lo, rel_g, rel_ref, lhs_ref, m_lhs, m_rel):
    step = pl.program_id(0)
    lanes = pl.ds(pl.multiple_of(step * CHUNK, CHUNK), CHUNK)
    packed = packed_ref[...]
    m_lhs[:, lanes] = onehot(lhs_of(packed), LOCAL)
    m_rel[:, lanes] = onehot(rel_of(packed), RELP)

    @pl.when(step == STEPS - 1)
    def _():
        for t in range(0, RELP // PER, 2):
            part = dot_t(rel_g[...], m_rel[t * PER : (t + 2) * PER, :]).astype(BF)
            side, at = jnp.bitwise_xor(core_ref[0], t // 4), t % 4
            rel_ref[side, at, 0:D, :] = part[:, 0:PER]
            rel_ref[side, at + 1, 0:D, :] = part[:, PER:]
            rel_ref[side, at, D:512, :] = jnp.zeros((112, PER), BF)
            rel_ref[side, at + 1, D:512, :] = jnp.zeros((112, PER), BF)
        lhs_ref[...] = dot_t(lhs_g[...], m_lhs[...]) + dot_t(lhs_lo[...], m_lhs[...])


def sums(core, packed, lhs_g, lhs_lo, rel_g):
    whole = lambda shape: pl.BlockSpec(shape, lambda i, p: (0,) * len(shape))
    return pl.pallas_call(
        sums_kernel,
        grid_spec=pltpu.PrefetchScalarGridSpec(
            num_scalar_prefetch=1,
            grid=(STEPS,),
            in_specs=[pl.BlockSpec((1, CHUNK), lambda i, p: (0, i))] + [whole((D, EDGES))] * 3,
            out_specs=[whole((2, 4, 512, PER)), whole((D, LOCAL))],
            scratch_shapes=[pltpu.VMEM((LOCAL, EDGES), BF), pltpu.VMEM((RELP, EDGES), BF)],
        ),
        out_shape=[
            jax.ShapeDtypeStruct((2, 4, 512, PER), BF),
            jax.ShapeDtypeStruct((D, LOCAL), F32),
        ],
        compiler_params=pltpu.CompilerParams(vmem_limit_bytes=58 * MIB),
        cost_estimate=pl.CostEstimate(flops=3_000_000_000, bytes_accessed=6_000_000, transcendentals=0),
        name="edge_sums",
    )(core, packed, lhs_g, lhs_lo, rel_g)


def total_kernel(parts_ref, out_ref):
    total = jnp.sum(parts_ref[...].astype(F32), 0).astype(BF)
    out_ref[...] = jnp.broadcast_to(total[None], out_ref.shape)


def total_for_all(parts):
    return pl.pallas_call(
        total_kernel,
        out_shape=jax.ShapeDtypeStruct(parts.shape, BF),
        name="total_for_all",
    )(parts)


def adagrad(table, accum, grad):
    new_accum = accum + jnp.mean(grad * grad, 0, keepdims=True)
    return table - grad * (LEARN / (jnp.sqrt(new_accum) + TINY)), new_accum


def right_kernel(partner_ref, ext_ref, back_ref, new_ref, accum_ref, pos, neg, m_pos, m_one, m_two):
    del partner_ref
    for s in range(OWNERS):
        lanes = slice(s * PER, (s + 1) * PER)
        pos[:, lanes] = back_ref[s, 0:D, :]
        neg[:, lanes] = back_ref[s, D:SEND, :]
        named = back_ref[s, SEND:BACK, :].astype(F32).astype(jnp.int32)
        m_pos[:, lanes] = onehot(named[0:1], LOCAL)
        m_one[:, lanes], m_two[:, lanes] = fold_marks(onehot(named[1:2], LOCAL))
    low = dot_t(neg[...], m_two[...])[0 : D - FOLD]
    grad = dot_t(pos[...], m_pos[...]) + jnp.concatenate([dot_t(neg[...], m_one[...]), low], 0)
    new_ref[...], accum_ref[...] = adagrad(ext_ref[0, 0:D, :], ext_ref[0, D : D + 1, :], grad)


def right_update(partner, ext_all, back):
    whole = lambda shape: pl.BlockSpec(shape, lambda i, p: (0,) * len(shape))
    marks = pltpu.VMEM((LOCAL, OWNERS * PER), BF)
    return pl.pallas_call(
        right_kernel,
        grid_spec=pltpu.PrefetchScalarGridSpec(
            num_scalar_prefetch=1,
            grid=(1,),
            in_specs=[
                pl.BlockSpec((1, D + 8, LOCAL), lambda i, p: (p[0], 0, 0)),
                whole((OWNERS, BACK, PER)),
            ],
            out_specs=[whole((D, LOCAL)), whole((1, LOCAL))],
            scratch_shapes=[
                pltpu.VMEM((D, OWNERS * PER), BF),
                pltpu.VMEM((FOLD, OWNERS * PER), BF),
                marks,
                marks,
                marks,
            ],
        ),
        out_shape=[jax.ShapeDtypeStruct((D, LOCAL), F32), jax.ShapeDtypeStruct((1, LOCAL), F32)],
        compiler_params=pltpu.CompilerParams(vmem_limit_bytes=20 * MIB),
        cost_estimate=pl.CostEstimate(flops=2_000_000_000, bytes_accessed=5_000_000, transcendentals=0),
        name="right_update",
    )(partner, ext_all, back)


def left_kernel(table_ref, accum_ref, grad_ref, new_ref, new_accum_ref):
    new_ref[...], new_accum_ref[...] = adagrad(table_ref[...], accum_ref[...], grad_ref[...])


def left_update(table, accum, grad):
    return pl.pallas_call(
        left_kernel,
        out_shape=[jax.ShapeDtypeStruct((D, LOCAL), F32), jax.ShapeDtypeStruct((1, LOCAL), F32)],
        name="left_update",
    )(table, accum, grad)


def relation_kernel(core_ref, table_ref, accum_ref, own_ref, other_ref, new_ref, new_accum_ref):
    owned = pl.program_id(0) // 2 == core_ref[0]
    first, second = jnp.where(owned, own_ref[0, 0:D, :], other_ref[0, 0:D, :]), jnp.where(owned, own_ref[1, 0:D, :], other_ref[1, 0:D, :])
    grad = jnp.concatenate([first, second], 1).astype(F32)
    new_ref[...], new_accum_ref[...] = adagrad(table_ref[...], accum_ref[...], grad)


def relation_update(core, table, accum, own, other):
    tall = pl.BlockSpec((D, 2 * PER), lambda i, p: (0, i))
    flat = pl.BlockSpec((1, 2 * PER), lambda i, p: (0, i))
    half = pl.BlockSpec((2, 512, PER), lambda i, p: (i % 2, 0, 0))
    return pl.pallas_call(
        relation_kernel,
        grid_spec=pltpu.PrefetchScalarGridSpec(
            num_scalar_prefetch=1,
            grid=(4,),
            in_specs=[tall, flat, half, half],
            out_specs=[tall, flat],
        ),
        out_shape=[jax.ShapeDtypeStruct((D, REL), F32), jax.ShapeDtypeStruct((1, REL), F32)],
        name="relation_update",
    )(core, table, accum, own, other)


CORES = [(0, 1), (1, 0)]
GRP, ROW, CHIPS = ("x", "core"), ("z", "y"), ("x", "z", "y")


def shift(value, axis, distance):
    return lax.ppermute(value, axis, [(i, (i + distance) & 3) for i in range(4)])


def other_core(value):
    return lax.ppermute(value, "core", CORES)


def pick(near, target, group):
    back = ((group >> 1) - (target >> 1)) & 3
    return jnp.where(back < 2, jnp.where(back == 0, near[0], near[1]), jnp.where(back == 2, near[2], near[3]))


def relative(owner, z, y):
    return (((z - (owner >> 2)) & 3) << 2) | ((y - (owner & 3)) & 3)


def gather_rows(first, second):
    lines = [[first] + [shift(first, "y", d) for d in (2, 1, 3)], [second] + [shift(second, "z", d) for d in (2, 1, 3)]]
    (f0, f2, f1, f3), (s0, s2, s1, s3) = lax.optimization_barrier(lines)
    first, second = jnp.stack([f0, f1, f2, f3]), jnp.stack([s0, s1, s2, s3])
    f2, s2 = shift(first, "z", 2), shift(second, "y", 2)
    f1, s1 = shift(first, "z", 1), shift(second, "y", 1)
    f3, s3 = shift(first, "z", 3), shift(second, "y", 3)
    return [first, f1, f2, f3, second, s1, s2, s3]


def body(
    lhs_emb,
    lhs_accum,
    rhs_emb,
    rhs_accum,
    rel_emb,
    rel_accum,
    partner,
    edge_lhs,
    edge_rhs,
    edge_rel,
    edge_count,
    neg_rhs,
):
    lhs_t, rhs_t, rel_t = lhs_emb[0].T, rhs_emb[0].T, rel_emb.T
    core, z, y = lax.axis_index("core"), lax.axis_index("z"), lax.axis_index("y")
    group = 2 * lax.axis_index("x") + core

    mine = rhs_t.astype(BF)
    target = partner[0]
    other = other_core(partner)[0]
    near = [mine] + [shift(mine, "x", d) for d in (1, 2, 3)]
    here = pick(near, target, group)
    across = other_core(pick(near, other, group))
    held = jnp.where((target & 1) == (group & 1), here, across)
    order = jnp.arange(OWNERS, dtype=jnp.int32)
    place = relative(order, z, y)
    live = (jnp.arange(EDGES, dtype=jnp.int32) < edge_count[0, 0]).astype(jnp.int32)
    pos_key = (relative(edge_rhs[0, 0] >> 8, z, y) << 27) | ((edge_rhs[0, 0] & (LOCAL - 1)) << 19)
    pos_key = pos_key | (edge_rel[0, 0] << 9) | (edge_lhs[0, 0] << 1) | live
    neg_key = (relative(neg_rhs[0, 0] >> 8, z, y) << 8) | (neg_rhs[0, 0] & (LOCAL - 1))
    spare = jnp.full((EDGES - NEG,), 1 << 30, jnp.int32)
    keys = jnp.stack([pos_key, jnp.concatenate([neg_key, spare])])
    exact = jnp.concatenate([rhs_t, jnp.broadcast_to(rhs_accum, (8, LOCAL))], 0)
    exact, held, keys = lax.optimization_barrier((exact, held, keys))
    ext_all = lax.all_gather(exact, GRP, axis=0, tiled=False)
    halves = gather_rows(held[:, :PER], held[:, PER:])
    packed, neg_index = lax.sort(keys, is_stable=False)
    neg_index = neg_index[:NEG].reshape(STEPS, PER)
    packed = packed.reshape(1, EDGES)
    left, weight, query = make_query(packed, lhs_t, rel_t)

    back, lhs_g, lhs_lo, rel_g = edges(place, packed, neg_index, halves, query, left, weight)
    returned = lax.all_to_all(back, ROW, 0, 0, tiled=True)
    at_core = core.astype(jnp.int32).reshape(1)
    rel_sums, lhs_sum = sums(at_core, packed, lhs_g, lhs_lo, rel_g)
    rel_sum = (rel_sums[0].astype(F32) + other_core(rel_sums[1]).astype(F32)).astype(BF)
    rel_sum, returned = lax.optimization_barrier((rel_sum, returned))
    parts = lax.all_to_all(rel_sum.reshape(64, 32, PER), CHIPS, 0, 0, tiled=True)
    own = lax.all_to_all(total_for_all(parts), CHIPS, 0, 0, tiled=True).reshape(4, 512, PER)

    new_lhs, new_lhs_accum = left_update(lhs_t, lhs_accum, lhs_sum)
    new_rhs, new_rhs_accum = right_update(partner, ext_all, returned)
    own, new_rhs = lax.optimization_barrier((own, new_rhs))
    new_rel, new_rel_accum = relation_update(at_core, rel_t, rel_accum[None], own, other_core(own))
    return (
        new_lhs.T[None],
        new_lhs_accum,
        new_rhs.T[None],
        new_rhs_accum,
        new_rel.T,
        new_rel_accum[0],
    )


def solution(mesh):
    fine = jax.sharding.Mesh(mesh.devices.reshape(4, 2, 4, 4), ("x", "core", "z", "y"))
    rows = P(GRP, ROW, None)
    in_specs = (rows, P(GRP, ROW), rows, P(GRP, ROW), P(), P(), P(GRP), rows, rows, rows, P(GRP, ROW), rows)
    out_specs = (rows, P(GRP, ROW), rows, P(GRP, ROW), P(), P())
    return jax.shard_map(body, mesh=fine, in_specs=in_specs, out_specs=out_specs, check_vma=False)
```

```python
import functools

import jax
import jax.numpy as jnp
from jax import lax
from jax.experimental import pallas as pl
from jax.experimental.pallas import tpu as pltpu
from jax.sharding import PartitionSpec as P

LEARN = 0.25
TINY = 1e-10
BF = jnp.bfloat16
F32 = jnp.float32
D = 400
HALF = 200
SECOND = 208
TALL = 2 * SECOND
REL = 1000
RELP = 1024
LOCAL = 256
EDGES = 2048
NEG = 1024
OWNERS = 16
PER = 128
FOLD = 208
SEND = D + FOLD
BACK = SEND + 16
CHUNK = 256
STEPS = EDGES // CHUNK
MIB = 1024 * 1024


def onehot(index, count):
    rows = lax.broadcasted_iota(jnp.int32, (count, index.shape[1]), 0)
    return jnp.where(rows == index, 1.0, 0.0).astype(BF)


def dot(a, b):
    return jnp.dot(a, b, preferred_element_type=F32)


def dot_t(a, b):
    return lax.dot_general(a, b, (((1,), (1,)), ((), ())), preferred_element_type=F32)


def split(value):
    high = value.astype(BF)
    return high, (value - high.astype(F32)).astype(BF)


def lhs_of(packed):
    return jnp.bitwise_and(jnp.right_shift(packed, 1), LOCAL - 1)


def rel_of(packed):
    return jnp.bitwise_and(jnp.right_shift(packed, 9), RELP - 1)


def query_kernel(keys_ref, lhs_ref, rel_ref, l_ref, w_ref, q_ref, lhs_two, rel_two):
    @pl.when(pl.program_id(0) == 0)
    def _():
        high, low = split(lhs_ref[...])
        lhs_two[0:D, :] = high
        lhs_two[D : 2 * D, :] = low
        rel_two[...] = jnp.zeros_like(rel_two)
        high, low = split(rel_ref[...])
        rel_two[0:D, 0:REL] = high
        rel_two[D : 2 * D, 0:REL] = low

    packed = keys_ref[0:1, :]
    both = dot(lhs_two[...], onehot(lhs_of(packed), LOCAL))
    left = both[0:D] + both[D : 2 * D]
    both = dot(rel_two[...], onehot(rel_of(packed), RELP))
    weight = both[0:D] + both[D : 2 * D]
    none = jnp.zeros((SECOND - HALF, CHUNK), F32)
    l_ref[...] = jnp.concatenate([left[:HALF], none, left[HALF:], none], 0).astype(BF)
    w_ref[...] = jnp.concatenate([weight[:HALF], none, weight[HALF:], none], 0).astype(BF)
    la, lb, wa, wb = left[:HALF], left[HALF:], weight[:HALF], weight[HALF:]
    q_ref[...] = jnp.concatenate([la * wa - lb * wb, la * wb + lb * wa], 0).astype(BF)


def make_query(keys, lhs_t, rel_t):
    wide = pl.BlockSpec((D, CHUNK), lambda i: (0, i))
    tall = pl.BlockSpec((TALL, CHUNK), lambda i: (0, i))
    return pl.pallas_call(
        query_kernel,
        grid=(STEPS,),
        in_specs=[
            pl.BlockSpec((2, CHUNK), lambda i: (0, i)),
            pl.BlockSpec((D, LOCAL), lambda i: (0, 0)),
            pl.BlockSpec((D, REL), lambda i: (0, 0)),
        ],
        out_specs=[tall, tall, wide],
        out_shape=[
            jax.ShapeDtypeStruct((TALL, EDGES), BF),
            jax.ShapeDtypeStruct((TALL, EDGES), BF),
            jax.ShapeDtypeStruct((D, EDGES), BF),
        ],
        scratch_shapes=[pltpu.VMEM((2 * D, LOCAL), BF), pltpu.VMEM((2 * D, RELP), BF)],
        compiler_params=pltpu.CompilerParams(vmem_limit_bytes=58 * MIB),
        cost_estimate=pl.CostEstimate(flops=5_000_000_000, bytes_accessed=10_000_000, transcendentals=0),
        name="make_query",
    )(keys, lhs_t, rel_t)


def fold_marks(marks):
    first = lax.broadcasted_iota(jnp.int32, marks.shape, 1) < 64
    none = jnp.zeros_like(marks)
    return jnp.where(first, marks, none), jnp.where(first, none, marks)


def twice(row):
    first = lax.broadcasted_iota(jnp.int32, row.shape, 1) < 64
    turned = pltpu.roll(row, 64, 1)
    return jnp.where(first, row, turned), jnp.where(first, turned, row)


def labels(pos, neg):
    row = lax.broadcasted_iota(jnp.int32, (16, PER), 0)
    return jnp.where(row == 0, pos, jnp.where(row == 1, neg, 0)).astype(F32).astype(BF)


def edge_kernel(
    place_ref, keys_ref, a0, a1, a2, a3, b0, b1, b2, b3, q_hbm, l_hbm, w_hbm, back_hbm, lhs_hbm, rel_hbm,
    table, neg_t, neg_n, weights, q_ref, l_ref, w_ref, back_ref, lhs_g, rel_g, scores, pos, grad, sems,
):
    count = iter(range(COPIES))

    def move(source, target):
        copy = pltpu.make_async_copy(source, target, sems.at[next(count)])
        copy.start()
        return copy

    blocks, loads = [], []
    for z, a in enumerate((a0, a1, a2, a3)):
        for y, b in enumerate((b0, b1, b2, b3)):
            at = 4 * z + y
            blocks.append((move(a.at[y], table.at[at, :, 0:PER]), move(b.at[z], table.at[at, :, PER:LOCAL])))
    for hbm, ref in ((q_hbm, q_ref), (l_hbm, l_ref), (w_hbm, w_ref)):
        loads.append(move(hbm, ref))
    for pair in blocks:
        for copy in pair:
            copy.wait()

    for c in range(STEPS):
        here = jnp.bitwise_and(keys_ref[1:2, c * PER : (c + 1) * PER], LOCAL - 1)
        one, two = fold_marks(onehot(here, LOCAL))
        rows = dot(table[2 * c], one) + dot(table[2 * c + 1], two)
        lanes = slice(c * PER, (c + 1) * PER)
        neg_t[:, lanes] = rows.astype(BF)
        neg_n[lanes, :] = rows.T.astype(BF)

    loads[0].wait()
    for part in range(STEPS):
        h = part % BUFFERS
        lanes = own = slice(part * CHUNK, (part + 1) * CHUNK)
        packed = keys_ref[0:1, lanes]
        live = jnp.bitwise_and(packed, 1).astype(F32)
        query = q_ref[:, own]
        asked = jnp.bitwise_and(jnp.right_shift(packed, 19), LOCAL - 1)
        marks = onehot(asked, LOCAL)
        scores[h] = dot(neg_n[...], query)
        pos[h, :, 0:PER] = dot(table[2 * part], marks[:, 0:PER])
        pos[h, :, PER:] = dot(table[2 * part + 1], marks[:, PER:])
        pos_score = jnp.zeros((8, CHUNK), F32)
        for r in range(0, D, 80):
            product = q_ref[r : r + 80, own].astype(F32) * pos[h, r : r + 80]
            pos_score = pos_score + jnp.sum(product.reshape(10, 8, CHUNK), 0)
        pos_score = jnp.sum(pos_score, 0, keepdims=True)
        highest = jnp.broadcast_to(pos_score, (8, CHUNK))
        for r in range(0, NEG, 64):
            highest = jnp.maximum(highest, jnp.max(scores[h, r : r + 64].reshape(8, 8, CHUNK), 0))
        highest = jnp.max(highest, 0, keepdims=True)
        total = jnp.zeros((8, CHUNK), F32)
        for r in range(0, NEG, 64):
            neg_exp = jnp.exp(scores[h, r : r + 64] - highest)
            total = total + jnp.sum(neg_exp.reshape(8, 8, CHUNK), 0)
            scores[h, r : r + 64] = neg_exp
        pos_exp = jnp.exp(pos_score - highest)
        total = pos_exp + jnp.sum(total, 0, keepdims=True)
        pos_weight = live * (pos_exp / total - 1.0)
        scale = live / total
        for r in range(0, NEG, 64):
            weights[r : r + 64, lanes] = (scores[h, r : r + 64] * scale).astype(BF)
        grad[h] = dot(neg_t[...], weights[:, lanes])
        one, two = twice(jnp.bitwise_and(keys_ref[1:2, part * PER : (part + 1) * PER], LOCAL - 1))
        k, m = place_ref[2 * part], place_ref[2 * part + 1]
        back_ref[k, SEND:BACK, :] = labels(asked[:, 0:PER], one)
        back_ref[m, SEND:BACK, :] = labels(asked[:, PER:], two)
        for r in range(0, D, 80):
            pos_grad = (pos_weight * q_ref[r : r + 80, own].astype(F32)).astype(BF)
            back_ref[k, r : r + 80, :] = pos_grad[:, 0:PER]
            back_ref[m, r : r + 80, :] = pos_grad[:, PER:]
        if part == 0:
            loads[1].wait()
            loads[2].wait()
        for r in range(0, HALF, 48):
            n, e = min(48, HALF - r), min(48, SECOND - r)
            ga = grad[h, r : r + n] + pos_weight * pos[h, r : r + n]
            gb = grad[h, HALF + r : HALF + r + n] + pos_weight * pos[h, HALF + r : HALF + r + n]
            if e > n:
                none = jnp.zeros((e - n, CHUNK), F32)
                ga, gb = jnp.concatenate([ga, none], 0), jnp.concatenate([gb, none], 0)
            for factor, out in ((w_ref, lhs_g), (l_ref, rel_g)):
                fa = factor[r : r + e, own].astype(F32)
                fb = factor[SECOND + r : SECOND + r + e, own].astype(F32)
                out[r : r + e, own] = (ga * fa + gb * fb).astype(BF)
                out[SECOND + r : SECOND + r + e, own] = (gb * fa - ga * fb).astype(BF)

    stores = [move(back_ref.at[:, 0:D], back_hbm.at[:, 0:D]), move(rel_g, rel_hbm), move(lhs_g, lhs_hbm)]
    for c in range(0, STEPS, 2):
        part = dot_t(q_ref[...], weights[c * PER : (c + 2) * PER, :])
        for h in (0, 1):
            both = part[:, h * PER : (h + 1) * PER]
            top = both[0:FOLD]
            low = jnp.concatenate([both[FOLD:D], jnp.zeros((2 * FOLD - D, PER), F32)], 0)
            first = lax.broadcasted_iota(jnp.int32, top.shape, 1) < 64
            k, m = place_ref[2 * (c + h)], place_ref[2 * (c + h) + 1]
            back_ref[k, D:SEND, :] = jnp.where(first, top, pltpu.roll(low, 64, 1)).astype(BF)
            back_ref[m, D:SEND, :] = jnp.where(first, pltpu.roll(top, 64, 1), low).astype(BF)
    stores.append(move(back_ref.at[:, D:BACK], back_hbm.at[:, D:BACK]))
    for copy in stores:
        copy.wait()


BUFFERS = 4
COPIES = 2 * OWNERS + 7


def edges(place, keys, halves, query, left, weight):
    anywhere = pl.BlockSpec(memory_space=pl.ANY)
    return pl.pallas_call(
        edge_kernel,
        in_specs=[pl.BlockSpec(memory_space=pltpu.SMEM), pl.BlockSpec(memory_space=pltpu.VMEM)] + [anywhere] * 11,
        out_specs=[anywhere] * 3,
        out_shape=[
            jax.ShapeDtypeStruct((OWNERS, BACK, PER), BF),
            jax.ShapeDtypeStruct((TALL, EDGES), BF),
            jax.ShapeDtypeStruct((TALL, EDGES), BF),
        ],
        scratch_shapes=[
            pltpu.VMEM((OWNERS, D, LOCAL), BF),
            pltpu.VMEM((D, NEG), BF),
            pltpu.VMEM((NEG, D), BF),
            pltpu.VMEM((NEG, EDGES), BF),
            pltpu.VMEM((D, EDGES), BF),
            pltpu.VMEM((TALL, EDGES), BF),
            pltpu.VMEM((TALL, EDGES), BF),
            pltpu.VMEM((OWNERS, BACK, PER), BF),
            pltpu.VMEM((TALL, EDGES), BF),
            pltpu.VMEM((TALL, EDGES), BF),
            pltpu.VMEM((BUFFERS, NEG, CHUNK), F32),
            pltpu.VMEM((BUFFERS, D, CHUNK), F32),
            pltpu.VMEM((BUFFERS, D, CHUNK), F32),
            pltpu.SemaphoreType.DMA((COPIES,)),
        ],
        compiler_params=pltpu.CompilerParams(vmem_limit_bytes=58 * MIB),
        cost_estimate=pl.CostEstimate(flops=8_000_000_000, bytes_accessed=20_000_000, transcendentals=2_100_000),
        name="edges",
    )(place, keys, *halves, query, left, weight)


def sums_kernel(keys_ref, lhs_g, rel_g, own_ref, other_ref, lhs_ref, total):
    wide = 4 * PER
    for c in range(0, EDGES, wide):
        packed = keys_ref[0:1, c : c + wide]
        marks = onehot(rel_of(packed), RELP)
        for t in range(0, RELP, 2 * PER):
            part = dot_t(rel_g[:, c : c + wide], marks[t : t + 2 * PER])
            lanes = slice(t, t + 2 * PER)
            total[:, lanes] = part if c == 0 else total[:, lanes] + part
        part = dot_t(lhs_g[:, c : c + wide], onehot(lhs_of(packed), LOCAL))
        part = jnp.concatenate([part[:HALF], part[SECOND : SECOND + HALF]], 0)
        lhs_ref[...] = part if c == 0 else lhs_ref[...] + part
    own = pl.multiple_of(lax.axis_index("core") * (RELP // 2), RELP // 2)
    other = pl.multiple_of((1 - lax.axis_index("core")) * (RELP // 2), RELP // 2)
    for at in range(4):
        for ref, start in ((own_ref, own), (other_ref, other)):
            lanes = pl.ds(start + at * PER, PER)
            ref[at, 0:D, :] = jnp.concatenate([total[0:HALF, lanes], total[SECOND : SECOND + HALF, lanes]], 0).astype(BF)
            ref[at, D:512, :] = jnp.zeros((112, PER), BF)


def sums(keys, lhs_g, rel_g):
    return pl.pallas_call(
        sums_kernel,
        out_shape=[
            jax.ShapeDtypeStruct((4, 512, PER), BF),
            jax.ShapeDtypeStruct((4, 512, PER), BF),
            jax.ShapeDtypeStruct((D, LOCAL), F32),
        ],
        scratch_shapes=[pltpu.VMEM((TALL, RELP), F32)],
        compiler_params=pltpu.CompilerParams(vmem_limit_bytes=58 * MIB),
        cost_estimate=pl.CostEstimate(flops=3_000_000_000, bytes_accessed=6_000_000, transcendentals=0),
        name="edge_sums",
    )(keys, lhs_g, rel_g)


def spread_kernel(axis, *refs):
    ins, outs = refs[:-4], refs[-4:]
    n = outs[0].shape[0]
    for d in range(4):
        rows = pl.ds(jnp.bitwise_and(lax.axis_index(axis) + d, 3) * n, n)
        total = ins[0][rows].astype(F32)
        for ref in ins[1:]:
            total = total + ref[rows].astype(F32)
        outs[d][...] = total.astype(BF)


def spread(axis, parts):
    n = parts[0].shape[0]
    return pl.pallas_call(
        functools.partial(spread_kernel, axis),
        out_shape=[jax.ShapeDtypeStruct((n // 4, 32, PER), BF)] * 4,
        name="spread",
    )(*parts)


def add_four(parts):
    own, one, two, three = (part.astype(F32) for part in parts)
    return ((own + two) + (one + three)).astype(BF)


def adagrad(table, accum, grad):
    new_accum = accum + jnp.mean(grad * grad, 0, keepdims=True)
    return table - grad * (LEARN / (jnp.sqrt(new_accum) + TINY)), new_accum


def right_kernel(partner_ref, ext_ref, back_ref, new_ref, accum_ref, pos, neg, m_pos, m_one, m_two):
    del partner_ref
    for s in range(OWNERS):
        lanes = slice(s * PER, (s + 1) * PER)
        pos[:, lanes] = back_ref[s, 0:D, :]
        neg[:, lanes] = back_ref[s, D:SEND, :]
        named = back_ref[s, SEND:BACK, :].astype(F32).astype(jnp.int32)
        m_pos[:, lanes] = onehot(named[0:1], LOCAL)
        m_one[:, lanes], m_two[:, lanes] = fold_marks(onehot(named[1:2], LOCAL))
    low = dot_t(neg[...], m_two[...])[0 : D - FOLD]
    grad = dot_t(pos[...], m_pos[...]) + jnp.concatenate([dot_t(neg[...], m_one[...]), low], 0)
    new_ref[...], accum_ref[...] = adagrad(ext_ref[0, 0:D, :], ext_ref[0, D : D + 1, :], grad)


def right_update(partner, ext_all, back):
    whole = lambda shape: pl.BlockSpec(shape, lambda i, p: (0,) * len(shape))
    marks = pltpu.VMEM((LOCAL, OWNERS * PER), BF)
    return pl.pallas_call(
        right_kernel,
        grid_spec=pltpu.PrefetchScalarGridSpec(
            num_scalar_prefetch=1,
            grid=(1,),
            in_specs=[
                pl.BlockSpec((1, D + 8, LOCAL), lambda i, p: (p[0], 0, 0)),
                whole((OWNERS, BACK, PER)),
            ],
            out_specs=[whole((D, LOCAL)), whole((1, LOCAL))],
            scratch_shapes=[
                pltpu.VMEM((D, OWNERS * PER), BF),
                pltpu.VMEM((FOLD, OWNERS * PER), BF),
                marks,
                marks,
                marks,
            ],
        ),
        out_shape=[jax.ShapeDtypeStruct((D, LOCAL), F32), jax.ShapeDtypeStruct((1, LOCAL), F32)],
        compiler_params=pltpu.CompilerParams(vmem_limit_bytes=20 * MIB),
        cost_estimate=pl.CostEstimate(flops=2_000_000_000, bytes_accessed=5_000_000, transcendentals=0),
        name="right_update",
    )(partner, ext_all, back)


def left_kernel(table_ref, accum_ref, grad_ref, new_ref, new_accum_ref):
    new_ref[...], new_accum_ref[...] = adagrad(table_ref[...], accum_ref[...], grad_ref[...])


def left_update(table, accum, grad):
    return pl.pallas_call(
        left_kernel,
        out_shape=[jax.ShapeDtypeStruct((D, LOCAL), F32), jax.ShapeDtypeStruct((1, LOCAL), F32)],
        name="left_update",
    )(table, accum, grad)


def relation_kernel(table_ref, accum_ref, own_ref, other_ref, new_ref, new_accum_ref):
    for t in range(RELP // PER):
        owned = lax.axis_index("core") == t // 4
        back = jnp.bitwise_and(lax.axis_index("x") - t, 3)
        lanes = slice(t * PER, min((t + 1) * PER, REL))
        grad = jnp.where(owned, own_ref[back, 0:D, :], other_ref[back, 0:D, :]).astype(F32)
        grad = grad[:, : lanes.stop - lanes.start]
        new_ref[:, lanes], new_accum_ref[:, lanes] = adagrad(table_ref[:, lanes], accum_ref[:, lanes], grad)


def relation_update(table, accum, own, other):
    return pl.pallas_call(
        relation_kernel,
        out_shape=[jax.ShapeDtypeStruct((D, REL), F32), jax.ShapeDtypeStruct((1, REL), F32)],
        name="relation_update",
    )(table, accum, own, other)


CORES = [(0, 1), (1, 0)]
GRP, ROW, CHIPS = ("x", "core"), ("z", "y"), ("x", "z", "y")


def shift(value, axis, distance):
    return lax.ppermute(value, axis, [(i, (i + distance) & 3) for i in range(4)])


def other_core(value):
    return lax.ppermute(value, "core", CORES)


def pick(near, target, group):
    back = ((group >> 1) - (target >> 1)) & 3
    return jnp.where(back < 2, jnp.where(back == 0, near[0], near[1]), jnp.where(back == 2, near[2], near[3]))


def relative(owner, z, y):
    return (((z - (owner >> 2)) & 3) << 2) | ((y - (owner & 3)) & 3)


def gather_rows(first, second):
    lines = [[first] + [shift(first, "y", d) for d in (2, 1, 3)], [second] + [shift(second, "z", d) for d in (2, 1, 3)]]
    (f0, f2, f1, f3), (s0, s2, s1, s3) = lax.optimization_barrier(lines)
    first, second = jnp.stack([f0, f1, f2, f3]), jnp.stack([s0, s1, s2, s3])
    f2, s2 = shift(first, "z", 2), shift(second, "y", 2)
    f1, s1 = shift(first, "z", 1), shift(second, "y", 1)
    f3, s3 = shift(first, "z", 3), shift(second, "y", 3)
    return [first, f1, f2, f3, second, s1, s2, s3]


def body(
    lhs_emb,
    lhs_accum,
    rhs_emb,
    rhs_accum,
    rel_emb,
    rel_accum,
    partner,
    edge_lhs,
    edge_rhs,
    edge_rel,
    edge_count,
    neg_rhs,
):
    lhs_t, rhs_t, rel_t = lhs_emb[0].T, rhs_emb[0].T, rel_emb.T
    x, core, z, y = (lax.axis_index(axis) for axis in ("x", "core", "z", "y"))
    group = 2 * x + core

    mine = rhs_t.astype(BF)
    target = partner[0]
    other = other_core(partner)[0]
    near = [mine] + [shift(mine, "x", d) for d in (1, 2, 3)]
    here = pick(near, target, group)
    across = other_core(pick(near, other, group))
    held = jnp.where((target & 1) == (group & 1), here, across)
    order = jnp.arange(OWNERS, dtype=jnp.int32)
    place = relative(order, z, y)
    live = (jnp.arange(EDGES, dtype=jnp.int32) < edge_count[0, 0]).astype(jnp.int32)
    pos_key = (relative(edge_rhs[0, 0] >> 8, z, y) << 27) | ((edge_rhs[0, 0] & (LOCAL - 1)) << 19)
    pos_key = pos_key | (edge_rel[0, 0] << 9) | (edge_lhs[0, 0] << 1) | live
    neg_key = (relative(neg_rhs[0, 0] >> 8, z, y) << 8) | (neg_rhs[0, 0] & (LOCAL - 1))
    spare = jnp.full((EDGES - NEG,), 1 << 30, jnp.int32)
    keys = jnp.stack([pos_key, jnp.concatenate([neg_key, spare])])
    exact = jnp.concatenate([rhs_t, jnp.broadcast_to(rhs_accum, (8, LOCAL))], 0)
    exact, held, keys, place = lax.optimization_barrier((exact, held, keys, place))
    ext_all = lax.all_gather(exact, GRP, axis=0, tiled=False)
    halves = gather_rows(held[:, :PER], held[:, PER:])
    keys = lax.sort(keys, is_stable=False)
    left, weight, query = make_query(keys, lhs_t, rel_t)

    back, lhs_g, rel_g = edges(place, keys, halves, query, left, weight)
    returned = lax.all_to_all(back, ROW, 0, 0, tiled=True)
    own, other, lhs_sum = sums(keys, lhs_g, rel_g)
    pieces = spread("x", [own.reshape(64, 32, PER), other_core(other).reshape(64, 32, PER)])
    total = add_four([pieces[0]] + [shift(pieces[d], "x", d) for d in (1, 2, 3)])
    for axis in ("z", "y"):
        total = add_four([total] + [shift(total, axis, d) for d in (1, 2, 3)])
    own = jnp.stack([total] + [shift(total, "x", d) for d in (1, 2, 3)]).reshape(4, 512, PER)

    new_lhs, new_lhs_accum = left_update(lhs_t, lhs_accum, lhs_sum)
    new_rhs, new_rhs_accum = right_update(partner, ext_all, returned)
    own, new_rhs, new_lhs = lax.optimization_barrier((own, new_rhs, new_lhs))
    new_rel, new_rel_accum = relation_update(rel_t, rel_accum[None], own, other_core(own))
    return (
        new_lhs.T[None],
        new_lhs_accum,
        new_rhs.T[None],
        new_rhs_accum,
        new_rel.T,
        new_rel_accum[0],
    )


def solution(mesh):
    fine = jax.sharding.Mesh(mesh.devices.reshape(4, 2, 4, 4), ("x", "core", "z", "y"))
    rows = P(GRP, ROW, None)
    in_specs = (rows, P(GRP, ROW), rows, P(GRP, ROW), P(), P(), P(GRP), rows, rows, rows, P(GRP, ROW), rows)
    out_specs = (rows, P(GRP, ROW), rows, P(GRP, ROW), P(), P())
    return jax.shard_map(body, mesh=fine, in_specs=in_specs, out_specs=out_specs, check_vma=False)
```

```python
import functools

import jax
import jax.numpy as jnp
from jax import lax
from jax.experimental import pallas as pl
from jax.experimental.pallas import tpu as pltpu
from jax.sharding import PartitionSpec as P

LEARN = 0.25
TINY = 1e-10
BF = jnp.bfloat16
F32 = jnp.float32
D = 400
HALF = 200
SECOND = 208
TALL = 2 * SECOND
REL = 1000
RELP = 1024
LOCAL = 256
EDGES = 2048
NEG = 1024
OWNERS = 16
PER = 128
FOLD = 208
SEND = D + FOLD
BACK = SEND + 16
CHUNK = 256
STEPS = EDGES // CHUNK
MIB = 1024 * 1024


def onehot(index, count):
    rows = lax.broadcasted_iota(jnp.int32, (count, index.shape[1]), 0)
    return jnp.where(rows == index, 1.0, 0.0).astype(BF)


def dot(a, b):
    return jnp.dot(a, b, preferred_element_type=F32)


def dot_t(a, b):
    return lax.dot_general(a, b, (((1,), (1,)), ((), ())), preferred_element_type=F32)


def split(value):
    high = value.astype(BF)
    return high, (value - high.astype(F32)).astype(BF)


def lhs_of(packed):
    return jnp.bitwise_and(jnp.right_shift(packed, 1), LOCAL - 1)


def rel_of(packed):
    return jnp.bitwise_and(jnp.right_shift(packed, 9), RELP - 1)


def query_kernel(keys_ref, lhs_ref, rel_ref, l_ref, w_ref, q_ref, lhs_two, rel_two):
    @pl.when(pl.program_id(0) == 0)
    def _():
        high, low = split(lhs_ref[...])
        lhs_two[0:D, :] = high
        lhs_two[D : 2 * D, :] = low
        rel_two[...] = jnp.zeros_like(rel_two)
        high, low = split(rel_ref[...])
        rel_two[0:D, 0:REL] = high
        rel_two[D : 2 * D, 0:REL] = low

    packed = keys_ref[0:1, :]
    both = dot(lhs_two[...], onehot(lhs_of(packed), LOCAL))
    left = both[0:D] + both[D : 2 * D]
    both = dot(rel_two[...], onehot(rel_of(packed), RELP))
    weight = both[0:D] + both[D : 2 * D]
    none = jnp.zeros((SECOND - HALF, CHUNK), F32)
    l_ref[...] = jnp.concatenate([left[:HALF], none, left[HALF:], none], 0).astype(BF)
    w_ref[...] = jnp.concatenate([weight[:HALF], none, weight[HALF:], none], 0).astype(BF)
    la, lb, wa, wb = left[:HALF], left[HALF:], weight[:HALF], weight[HALF:]
    q_ref[...] = jnp.concatenate([la * wa - lb * wb, la * wb + lb * wa], 0).astype(BF)


def make_query(keys, lhs_t, rel_t):
    wide = pl.BlockSpec((D, CHUNK), lambda i: (0, i))
    tall = pl.BlockSpec((TALL, CHUNK), lambda i: (0, i))
    return pl.pallas_call(
        query_kernel,
        grid=(STEPS,),
        in_specs=[
            pl.BlockSpec((2, CHUNK), lambda i: (0, i)),
            pl.BlockSpec((D, LOCAL), lambda i: (0, 0)),
            pl.BlockSpec((D, REL), lambda i: (0, 0)),
        ],
        out_specs=[tall, tall, wide],
        out_shape=[
            jax.ShapeDtypeStruct((TALL, EDGES), BF),
            jax.ShapeDtypeStruct((TALL, EDGES), BF),
            jax.ShapeDtypeStruct((D, EDGES), BF),
        ],
        scratch_shapes=[pltpu.VMEM((2 * D, LOCAL), BF), pltpu.VMEM((2 * D, RELP), BF)],
        compiler_params=pltpu.CompilerParams(vmem_limit_bytes=58 * MIB),
        cost_estimate=pl.CostEstimate(flops=5_000_000_000, bytes_accessed=10_000_000, transcendentals=0),
        name="make_query",
    )(keys, lhs_t, rel_t)


def fold_marks(marks):
    first = lax.broadcasted_iota(jnp.int32, marks.shape, 1) < 64
    none = jnp.zeros_like(marks)
    return jnp.where(first, marks, none), jnp.where(first, none, marks)


def twice(row):
    first = lax.broadcasted_iota(jnp.int32, row.shape, 1) < 64
    turned = pltpu.roll(row, 64, 1)
    return jnp.where(first, row, turned), jnp.where(first, turned, row)


def labels(pos, neg):
    row = lax.broadcasted_iota(jnp.int32, (16, PER), 0)
    return jnp.where(row == 0, pos, jnp.where(row == 1, neg, 0)).astype(F32).astype(BF)


def edge_kernel(
    place_ref, keys_ref, a0, a1, a2, a3, b0, b1, b2, b3, q_hbm, l_hbm, w_hbm, back_hbm, own_hbm, other_hbm, lhs_ref,
    table, neg_t, neg_n, weights, q_ref, l_ref, w_ref, back_ref, lhs_g, rel_g, scores, pos, grad, total_rel, own_ref, other_ref, sems,
):
    count = iter(range(COPIES))

    def move(source, target):
        copy = pltpu.make_async_copy(source, target, sems.at[next(count)])
        copy.start()
        return copy

    blocks, loads = [], []
    for z, a in enumerate((a0, a1, a2, a3)):
        for y, b in enumerate((b0, b1, b2, b3)):
            at = 4 * z + y
            blocks.append((move(a.at[y], table.at[at, :, 0:PER]), move(b.at[z], table.at[at, :, PER:LOCAL])))
    for hbm, ref in ((q_hbm, q_ref), (l_hbm, l_ref), (w_hbm, w_ref)):
        loads.append(move(hbm, ref))
    for pair in blocks:
        for copy in pair:
            copy.wait()

    for c in range(STEPS):
        here = jnp.bitwise_and(keys_ref[1:2, c * PER : (c + 1) * PER], LOCAL - 1)
        one, two = fold_marks(onehot(here, LOCAL))
        rows = dot(table[2 * c], one) + dot(table[2 * c + 1], two)
        lanes = slice(c * PER, (c + 1) * PER)
        neg_t[:, lanes] = rows.astype(BF)
        neg_n[lanes, :] = rows.T.astype(BF)

    loads[0].wait()
    for part in range(STEPS):
        h = part % BUFFERS
        lanes = own = slice(part * CHUNK, (part + 1) * CHUNK)
        packed = keys_ref[0:1, lanes]
        live = jnp.bitwise_and(packed, 1).astype(F32)
        query = q_ref[:, own]
        asked = jnp.bitwise_and(jnp.right_shift(packed, 19), LOCAL - 1)
        marks = onehot(asked, LOCAL)
        scores[h] = dot(neg_n[...], query)
        pos[h, :, 0:PER] = dot(table[2 * part], marks[:, 0:PER])
        pos[h, :, PER:] = dot(table[2 * part + 1], marks[:, PER:])
        pos_score = jnp.zeros((8, CHUNK), F32)
        for r in range(0, D, 80):
            product = q_ref[r : r + 80, own].astype(F32) * pos[h, r : r + 80]
            pos_score = pos_score + jnp.sum(product.reshape(10, 8, CHUNK), 0)
        pos_score = jnp.sum(pos_score, 0, keepdims=True)
        highest = jnp.broadcast_to(pos_score, (8, CHUNK))
        for r in range(0, NEG, 64):
            highest = jnp.maximum(highest, jnp.max(scores[h, r : r + 64].reshape(8, 8, CHUNK), 0))
        highest = jnp.max(highest, 0, keepdims=True)
        total = jnp.zeros((8, CHUNK), F32)
        for r in range(0, NEG, 64):
            neg_exp = jnp.exp(scores[h, r : r + 64] - highest)
            total = total + jnp.sum(neg_exp.reshape(8, 8, CHUNK), 0)
            scores[h, r : r + 64] = neg_exp
        pos_exp = jnp.exp(pos_score - highest)
        total = pos_exp + jnp.sum(total, 0, keepdims=True)
        pos_weight = live * (pos_exp / total - 1.0)
        scale = live / total
        for r in range(0, NEG, 64):
            weights[r : r + 64, lanes] = (scores[h, r : r + 64] * scale).astype(BF)
        grad[h] = dot(neg_t[...], weights[:, lanes])
        one, two = twice(jnp.bitwise_and(keys_ref[1:2, part * PER : (part + 1) * PER], LOCAL - 1))
        k, m = place_ref[2 * part], place_ref[2 * part + 1]
        back_ref[k, SEND:BACK, :] = labels(asked[:, 0:PER], one)
        back_ref[m, SEND:BACK, :] = labels(asked[:, PER:], two)
        for r in range(0, D, 80):
            pos_grad = (pos_weight * q_ref[r : r + 80, own].astype(F32)).astype(BF)
            back_ref[k, r : r + 80, :] = pos_grad[:, 0:PER]
            back_ref[m, r : r + 80, :] = pos_grad[:, PER:]
        if part == 0:
            loads[1].wait()
            loads[2].wait()
        for r in range(0, HALF, 48):
            n, e = min(48, HALF - r), min(48, SECOND - r)
            ga = grad[h, r : r + n] + pos_weight * pos[h, r : r + n]
            gb = grad[h, HALF + r : HALF + r + n] + pos_weight * pos[h, HALF + r : HALF + r + n]
            if e > n:
                none = jnp.zeros((e - n, CHUNK), F32)
                ga, gb = jnp.concatenate([ga, none], 0), jnp.concatenate([gb, none], 0)
            for factor, out in ((w_ref, lhs_g), (l_ref, rel_g)):
                fa = factor[r : r + e, own].astype(F32)
                fb = factor[SECOND + r : SECOND + r + e, own].astype(F32)
                out[r : r + e, own] = (ga * fa + gb * fb).astype(BF)
                out[SECOND + r : SECOND + r + e, own] = (gb * fa - ga * fb).astype(BF)

    stores = [move(back_ref.at[:, 0:D], back_hbm.at[:, 0:D])]
    wide = 4 * PER
    for c in range(0, EDGES, wide):
        packed = keys_ref[0:1, c : c + wide]
        marks = onehot(rel_of(packed), RELP)
        for t in range(0, RELP, 2 * PER):
            part = dot_t(rel_g[:, c : c + wide], marks[t : t + 2 * PER])
            lanes = slice(t, t + 2 * PER)
            total_rel[:, lanes] = part if c == 0 else total_rel[:, lanes] + part
    own = pl.multiple_of(lax.axis_index("core") * (RELP // 2), RELP // 2)
    other = pl.multiple_of((1 - lax.axis_index("core")) * (RELP // 2), RELP // 2)
    for ref, start, hbm in ((other_ref, other, other_hbm), (own_ref, own, own_hbm)):
        for at in range(4):
            lanes = pl.ds(start + at * PER, PER)
            both = jnp.concatenate([total_rel[0:HALF, lanes], total_rel[SECOND : SECOND + HALF, lanes]], 0)
            ref[at, 0:D, :] = both.astype(BF)
            ref[at, D:512, :] = jnp.zeros((512 - D, PER), BF)
        stores.append(move(ref, hbm))
    for c in range(0, EDGES, wide):
        marks = onehot(lhs_of(keys_ref[0:1, c : c + wide]), LOCAL)
        part = dot_t(lhs_g[:, c : c + wide], marks)
        part = jnp.concatenate([part[:HALF], part[SECOND : SECOND + HALF]], 0)
        lhs_ref[...] = part if c == 0 else lhs_ref[...] + part
    for c in range(0, STEPS, 2):
        part = dot_t(q_ref[...], weights[c * PER : (c + 2) * PER, :])
        for h in (0, 1):
            both = part[:, h * PER : (h + 1) * PER]
            top = both[0:FOLD]
            low = jnp.concatenate([both[FOLD:D], jnp.zeros((2 * FOLD - D, PER), F32)], 0)
            first = lax.broadcasted_iota(jnp.int32, top.shape, 1) < 64
            k, m = place_ref[2 * (c + h)], place_ref[2 * (c + h) + 1]
            back_ref[k, D:SEND, :] = jnp.where(first, top, pltpu.roll(low, 64, 1)).astype(BF)
            back_ref[m, D:SEND, :] = jnp.where(first, pltpu.roll(top, 64, 1), low).astype(BF)
    stores.append(move(back_ref.at[:, D:BACK], back_hbm.at[:, D:BACK]))
    for copy in stores:
        copy.wait()


BUFFERS = 4
COPIES = 2 * OWNERS + 7


def edges(place, keys, halves, query, left, weight):
    anywhere = pl.BlockSpec(memory_space=pl.ANY)
    return pl.pallas_call(
        edge_kernel,
        in_specs=[pl.BlockSpec(memory_space=pltpu.SMEM), pl.BlockSpec(memory_space=pltpu.VMEM)] + [anywhere] * 11,
        out_specs=[anywhere] * 3 + [pl.BlockSpec(memory_space=pltpu.VMEM)],
        out_shape=[
            jax.ShapeDtypeStruct((OWNERS, BACK, PER), BF),
            jax.ShapeDtypeStruct((4, 512, PER), BF),
            jax.ShapeDtypeStruct((4, 512, PER), BF),
            jax.ShapeDtypeStruct((D, LOCAL), F32),
        ],
        scratch_shapes=[
            pltpu.VMEM((OWNERS, D, LOCAL), BF),
            pltpu.VMEM((D, NEG), BF),
            pltpu.VMEM((NEG, D), BF),
            pltpu.VMEM((NEG, EDGES), BF),
            pltpu.VMEM((D, EDGES), BF),
            pltpu.VMEM((TALL, EDGES), BF),
            pltpu.VMEM((TALL, EDGES), BF),
            pltpu.VMEM((OWNERS, BACK, PER), BF),
            pltpu.VMEM((TALL, EDGES), BF),
            pltpu.VMEM((TALL, EDGES), BF),
            pltpu.VMEM((BUFFERS, NEG, CHUNK), F32),
            pltpu.VMEM((BUFFERS, D, CHUNK), F32),
            pltpu.VMEM((BUFFERS, D, CHUNK), F32),
            pltpu.VMEM((TALL, RELP), F32),
            pltpu.VMEM((4, 512, PER), BF),
            pltpu.VMEM((4, 512, PER), BF),
            pltpu.SemaphoreType.DMA((COPIES,)),
        ],
        compiler_params=pltpu.CompilerParams(vmem_limit_bytes=58 * MIB),
        cost_estimate=pl.CostEstimate(flops=8_000_000_000, bytes_accessed=20_000_000, transcendentals=2_100_000),
        name="edges",
    )(place, keys, *halves, query, left, weight)


def spread_kernel(axis, *refs):
    ins, outs = refs[:-4], refs[-4:]
    n = outs[0].shape[0]
    for d in range(4):
        rows = pl.ds(jnp.bitwise_and(lax.axis_index(axis) + d, 3) * n, n)
        total = ins[0][rows].astype(F32)
        for ref in ins[1:]:
            total = total + ref[rows].astype(F32)
        outs[d][...] = total.astype(BF)


def spread(axis, parts):
    n = parts[0].shape[0]
    return pl.pallas_call(
        functools.partial(spread_kernel, axis),
        out_shape=[jax.ShapeDtypeStruct((n // 4, 32, PER), BF)] * 4,
        name="spread",
    )(*parts)


def add_four(parts):
    own, one, two, three = (part.astype(F32) for part in parts)
    return ((own + two) + (one + three)).astype(BF)


def adagrad(table, accum, grad):
    new_accum = accum + jnp.mean(grad * grad, 0, keepdims=True)
    return table - grad * (LEARN / (jnp.sqrt(new_accum) + TINY)), new_accum


def right_kernel(partner_ref, ext_ref, back_ref, new_ref, accum_ref, pos, neg, m_pos, m_one, m_two):
    del partner_ref
    for s in range(OWNERS):
        lanes = slice(s * PER, (s + 1) * PER)
        pos[:, lanes] = back_ref[s, 0:D, :]
        neg[:, lanes] = back_ref[s, D:SEND, :]
        named = back_ref[s, SEND:BACK, :].astype(F32).astype(jnp.int32)
        m_pos[:, lanes] = onehot(named[0:1], LOCAL)
        m_one[:, lanes], m_two[:, lanes] = fold_marks(onehot(named[1:2], LOCAL))
    low = dot_t(neg[...], m_two[...])[0 : D - FOLD]
    grad = dot_t(pos[...], m_pos[...]) + jnp.concatenate([dot_t(neg[...], m_one[...]), low], 0)
    new_ref[...], accum_ref[...] = adagrad(ext_ref[0, 0:D, :], ext_ref[0, D : D + 1, :], grad)


def right_update(partner, ext_all, back):
    whole = lambda shape: pl.BlockSpec(shape, lambda i, p: (0,) * len(shape))
    marks = pltpu.VMEM((LOCAL, OWNERS * PER), BF)
    return pl.pallas_call(
        right_kernel,
        grid_spec=pltpu.PrefetchScalarGridSpec(
            num_scalar_prefetch=1,
            grid=(1,),
            in_specs=[
                pl.BlockSpec((1, D + 8, LOCAL), lambda i, p: (p[0], 0, 0)),
                whole((OWNERS, BACK, PER)),
            ],
            out_specs=[whole((D, LOCAL)), whole((1, LOCAL))],
            scratch_shapes=[
                pltpu.VMEM((D, OWNERS * PER), BF),
                pltpu.VMEM((FOLD, OWNERS * PER), BF),
                marks,
                marks,
                marks,
            ],
        ),
        out_shape=[jax.ShapeDtypeStruct((D, LOCAL), F32), jax.ShapeDtypeStruct((1, LOCAL), F32)],
        compiler_params=pltpu.CompilerParams(vmem_limit_bytes=58 * MIB),
        cost_estimate=pl.CostEstimate(flops=2_000_000_000, bytes_accessed=5_000_000, transcendentals=0),
        name="right_update",
    )(partner, ext_all, back)


def left_kernel(table_ref, accum_ref, grad_ref, new_ref, new_accum_ref):
    new_ref[...], new_accum_ref[...] = adagrad(table_ref[...], accum_ref[...], grad_ref[...])


def left_update(table, accum, grad):
    return pl.pallas_call(
        left_kernel,
        out_shape=[jax.ShapeDtypeStruct((D, LOCAL), F32), jax.ShapeDtypeStruct((1, LOCAL), F32)],
        name="left_update",
    )(table, accum, grad)


def relation_kernel(table_ref, accum_ref, own_ref, other_ref, new_ref, new_accum_ref):
    for t in range(RELP // PER):
        owned = lax.axis_index("core") == t // 4
        back = jnp.bitwise_and(lax.axis_index("x") - t, 3)
        lanes = slice(t * PER, min((t + 1) * PER, REL))
        grad = jnp.where(owned, own_ref[back, 0:D, :], other_ref[back, 0:D, :]).astype(F32)
        grad = grad[:, : lanes.stop - lanes.start]
        new_ref[:, lanes], new_accum_ref[:, lanes] = adagrad(table_ref[:, lanes], accum_ref[:, lanes], grad)


def relation_update(table, accum, own, other):
    return pl.pallas_call(
        relation_kernel,
        out_shape=[jax.ShapeDtypeStruct((D, REL), F32), jax.ShapeDtypeStruct((1, REL), F32)],
        compiler_params=pltpu.CompilerParams(vmem_limit_bytes=58 * MIB),
        name="relation_update",
    )(table, accum, own, other)


CORES = [(0, 1), (1, 0)]
GRP, ROW, CHIPS = ("x", "core"), ("z", "y"), ("x", "z", "y")


def shift(value, axis, distance):
    return lax.ppermute(value, axis, [(i, (i + distance) & 3) for i in range(4)])


def other_core(value):
    return lax.ppermute(value, "core", CORES)


def pick(near, target, group):
    back = ((group >> 1) - (target >> 1)) & 3
    return jnp.where(back < 2, jnp.where(back == 0, near[0], near[1]), jnp.where(back == 2, near[2], near[3]))


def relative(owner, z, y):
    return (((z - (owner >> 2)) & 3) << 2) | ((y - (owner & 3)) & 3)


def gather_rows(first, second):
    lines = [[first] + [shift(first, "y", d) for d in (2, 1, 3)], [second] + [shift(second, "z", d) for d in (2, 1, 3)]]
    (f0, f2, f1, f3), (s0, s2, s1, s3) = lax.optimization_barrier(lines)
    first, second = jnp.stack([f0, f1, f2, f3]), jnp.stack([s0, s1, s2, s3])
    f2, s2 = shift(first, "z", 2), shift(second, "y", 2)
    f1, s1 = shift(first, "z", 1), shift(second, "y", 1)
    f3, s3 = shift(first, "z", 3), shift(second, "y", 3)
    return [first, f1, f2, f3, second, s1, s2, s3]


def body(
    lhs_emb,
    lhs_accum,
    rhs_emb,
    rhs_accum,
    rel_emb,
    rel_accum,
    partner,
    edge_lhs,
    edge_rhs,
    edge_rel,
    edge_count,
    neg_rhs,
):
    lhs_t, rhs_t, rel_t = lhs_emb[0].T, rhs_emb[0].T, rel_emb.T
    x, core, z, y = (lax.axis_index(axis) for axis in ("x", "core", "z", "y"))
    group = 2 * x + core

    mine = rhs_t.astype(BF)
    target = partner[0]
    other = other_core(partner)[0]
    near = [mine] + [shift(mine, "x", d) for d in (1, 2, 3)]
    here = pick(near, target, group)
    across = other_core(pick(near, other, group))
    held = jnp.where((target & 1) == (group & 1), here, across)
    order = jnp.arange(OWNERS, dtype=jnp.int32)
    place = relative(order, z, y)
    live = (jnp.arange(EDGES, dtype=jnp.int32) < edge_count[0, 0]).astype(jnp.int32)
    pos_key = (relative(edge_rhs[0, 0] >> 8, z, y) << 27) | ((edge_rhs[0, 0] & (LOCAL - 1)) << 19)
    pos_key = pos_key | (edge_rel[0, 0] << 9) | (edge_lhs[0, 0] << 1) | live
    neg_key = (relative(neg_rhs[0, 0] >> 8, z, y) << 8) | (neg_rhs[0, 0] & (LOCAL - 1))
    spare = jnp.full((EDGES - NEG,), 1 << 30, jnp.int32)
    keys = jnp.stack([pos_key, jnp.concatenate([neg_key, spare])])
    exact = jnp.concatenate([rhs_t, jnp.broadcast_to(rhs_accum, (8, LOCAL))], 0)
    exact, held, keys, place = lax.optimization_barrier((exact, held, keys, place))
    ext_all = lax.all_gather(exact, GRP, axis=0, tiled=False)
    halves = gather_rows(held[:, :PER], held[:, PER:])
    keys = lax.sort(keys, is_stable=False)
    left, weight, query = make_query(keys, lhs_t, rel_t)

    back, own, other, lhs_sum = edges(place, keys, halves, query, left, weight)
    returned = lax.all_to_all(back, ROW, 0, 0, tiled=True)
    new_lhs, new_lhs_accum = left_update(lhs_t, lhs_accum, lhs_sum)
    new_rhs, new_rhs_accum = right_update(partner, ext_all, returned)
    pieces = spread("x", [own.reshape(64, 32, PER), other_core(other).reshape(64, 32, PER)])
    total = add_four([pieces[0]] + [shift(pieces[d], "x", d) for d in (1, 2, 3)])
    total = add_four([total] + [shift(total, "z", d) for d in (1, 2, 3)])
    pieces = [total] + [shift(total, "y", d) for d in (1, 2, 3)]
    pieces, new_lhs, new_rhs = lax.optimization_barrier((pieces, new_lhs, new_rhs))
    total = add_four(pieces)
    pieces = [total] + [shift(total, "x", d) for d in (1, 2, 3)]
    own = jnp.stack(pieces).reshape(4, 512, PER)
    new_rel, new_rel_accum = relation_update(rel_t, rel_accum[None], own, other_core(own))
    return (
        new_lhs.T[None],
        new_lhs_accum,
        new_rhs.T[None],
        new_rhs_accum,
        new_rel.T,
        new_rel_accum[0],
    )


def solution(mesh):
    fine = jax.sharding.Mesh(mesh.devices.reshape(4, 2, 4, 4), ("x", "core", "z", "y"))
    rows = P(GRP, ROW, None)
    in_specs = (rows, P(GRP, ROW), rows, P(GRP, ROW), P(), P(), P(GRP), rows, rows, rows, P(GRP, ROW), rows)
    out_specs = (rows, P(GRP, ROW), rows, P(GRP, ROW), P(), P())
    return jax.shard_map(body, mesh=fine, in_specs=in_specs, out_specs=out_specs, check_vma=False)
```

```python
import functools

import jax
import jax.numpy as jnp
from jax import lax
from jax.experimental import pallas as pl
from jax.experimental.pallas import tpu as pltpu
from jax.sharding import PartitionSpec as P

LEARN = 0.25
TINY = 1e-10
BF = jnp.bfloat16
F32 = jnp.float32
D = 400
HALF = 200
SECOND = 208
TALL = 2 * SECOND
REL = 1000
RELP = 1024
LOCAL = 256
EDGES = 2048
NEG = 1024
OWNERS = 16
PER = 128
FOLD = 208
SEND = D + FOLD
BACK = SEND + 16
CHUNK = 256
STEPS = EDGES // CHUNK
MIB = 1024 * 1024


def onehot(index, count):
    rows = lax.broadcasted_iota(jnp.int32, (count, index.shape[1]), 0)
    return jnp.where(rows == index, 1.0, 0.0).astype(BF)


def dot(a, b):
    return jnp.dot(a, b, preferred_element_type=F32)


def dot_t(a, b):
    return lax.dot_general(a, b, (((1,), (1,)), ((), ())), preferred_element_type=F32)


def split(value):
    high = value.astype(BF)
    return high, (value - high.astype(F32)).astype(BF)


def lhs_of(packed):
    return jnp.bitwise_and(jnp.right_shift(packed, 1), LOCAL - 1)


def rel_of(packed):
    return jnp.bitwise_and(jnp.right_shift(packed, 9), RELP - 1)


def query_kernel(keys_ref, lhs_ref, rel_ref, l_ref, w_ref, q_ref, lhs_two, rel_two):
    @pl.when(pl.program_id(0) == 0)
    def _():
        high, low = split(lhs_ref[...])
        lhs_two[0:D, :] = high
        lhs_two[D : 2 * D, :] = low
        rel_two[...] = jnp.zeros_like(rel_two)
        high, low = split(rel_ref[...])
        rel_two[0:D, 0:REL] = high
        rel_two[D : 2 * D, 0:REL] = low

    packed = keys_ref[0:1, :]
    both = dot(lhs_two[...], onehot(lhs_of(packed), LOCAL))
    left = both[0:D] + both[D : 2 * D]
    both = dot(rel_two[...], onehot(rel_of(packed), RELP))
    weight = both[0:D] + both[D : 2 * D]
    none = jnp.zeros((SECOND - HALF, CHUNK), F32)
    l_ref[...] = jnp.concatenate([left[:HALF], none, left[HALF:], none], 0).astype(BF)
    w_ref[...] = jnp.concatenate([weight[:HALF], none, weight[HALF:], none], 0).astype(BF)
    la, lb, wa, wb = left[:HALF], left[HALF:], weight[:HALF], weight[HALF:]
    q_ref[...] = jnp.concatenate([la * wa - lb * wb, la * wb + lb * wa], 0).astype(BF)


def make_query(keys, lhs_t, rel_t):
    wide = pl.BlockSpec((D, CHUNK), lambda i: (0, i))
    tall = pl.BlockSpec((TALL, CHUNK), lambda i: (0, i))
    return pl.pallas_call(
        query_kernel,
        grid=(STEPS,),
        in_specs=[
            pl.BlockSpec((2, CHUNK), lambda i: (0, i)),
            pl.BlockSpec((D, LOCAL), lambda i: (0, 0)),
            pl.BlockSpec((D, REL), lambda i: (0, 0)),
        ],
        out_specs=[tall, tall, wide],
        out_shape=[
            jax.ShapeDtypeStruct((TALL, EDGES), BF),
            jax.ShapeDtypeStruct((TALL, EDGES), BF),
            jax.ShapeDtypeStruct((D, EDGES), BF),
        ],
        scratch_shapes=[pltpu.VMEM((2 * D, LOCAL), BF), pltpu.VMEM((2 * D, RELP), BF)],
        compiler_params=pltpu.CompilerParams(vmem_limit_bytes=58 * MIB),
        cost_estimate=pl.CostEstimate(flops=5_000_000_000, bytes_accessed=10_000_000, transcendentals=0),
        name="make_query",
    )(keys, lhs_t, rel_t)


def fold_marks(marks):
    first = lax.broadcasted_iota(jnp.int32, marks.shape, 1) < 64
    none = jnp.zeros_like(marks)
    return jnp.where(first, marks, none), jnp.where(first, none, marks)


def twice(row):
    first = lax.broadcasted_iota(jnp.int32, row.shape, 1) < 64
    turned = pltpu.roll(row, 64, 1)
    return jnp.where(first, row, turned), jnp.where(first, turned, row)


def labels(pos, neg):
    row = lax.broadcasted_iota(jnp.int32, (16, PER), 0)
    return jnp.where(row == 0, pos, jnp.where(row == 1, neg, 0)).astype(F32).astype(BF)


def edge_kernel(
    place_ref, keys_ref, a0, a1, a2, a3, b0, b1, b2, b3, q_hbm, l_hbm, w_hbm, back_hbm, own_hbm, other_hbm, lhs_ref,
    table, neg_t, neg_n, weights, q_ref, l_ref, w_ref, back_ref, lhs_g, rel_g, scores, pos, grad, total_rel, own_ref, other_ref, sems,
):
    count = iter(range(COPIES))

    def move(source, target):
        copy = pltpu.make_async_copy(source, target, sems.at[next(count)])
        copy.start()
        return copy

    blocks, loads = [], []
    for z, a in enumerate((a0, a1, a2, a3)):
        for y, b in enumerate((b0, b1, b2, b3)):
            at = 4 * z + y
            blocks.append((move(a.at[y], table.at[at, :, 0:PER]), move(b.at[z], table.at[at, :, PER:LOCAL])))
    for hbm, ref in ((q_hbm, q_ref), (l_hbm, l_ref), (w_hbm, w_ref)):
        loads.append(move(hbm, ref))
    for pair in blocks:
        for copy in pair:
            copy.wait()

    for c in range(STEPS):
        here = jnp.bitwise_and(keys_ref[1:2, c * PER : (c + 1) * PER], LOCAL - 1)
        one, two = fold_marks(onehot(here, LOCAL))
        rows = dot(table[2 * c], one) + dot(table[2 * c + 1], two)
        lanes = slice(c * PER, (c + 1) * PER)
        neg_t[:, lanes] = rows.astype(BF)
        neg_n[lanes, :] = rows.T.astype(BF)

    loads[0].wait()
    for part in range(STEPS):
        h = part % BUFFERS
        lanes = own = slice(part * CHUNK, (part + 1) * CHUNK)
        packed = keys_ref[0:1, lanes]
        live = jnp.bitwise_and(packed, 1).astype(F32)
        query = q_ref[:, own]
        asked = jnp.bitwise_and(jnp.right_shift(packed, 19), LOCAL - 1)
        marks = onehot(asked, LOCAL)
        scores[h] = dot(neg_n[...], query)
        pos[h, :, 0:PER] = dot(table[2 * part], marks[:, 0:PER])
        pos[h, :, PER:] = dot(table[2 * part + 1], marks[:, PER:])
        pos_score = jnp.zeros((8, CHUNK), F32)
        for r in range(0, D, 80):
            product = q_ref[r : r + 80, own].astype(F32) * pos[h, r : r + 80]
            pos_score = pos_score + jnp.sum(product.reshape(10, 8, CHUNK), 0)
        pos_score = jnp.sum(pos_score, 0, keepdims=True)
        highest = jnp.broadcast_to(pos_score, (8, CHUNK))
        for r in range(0, NEG, 64):
            highest = jnp.maximum(highest, jnp.max(scores[h, r : r + 64].reshape(8, 8, CHUNK), 0))
        highest = jnp.max(highest, 0, keepdims=True)
        total = jnp.zeros((8, CHUNK), F32)
        for r in range(0, NEG, 64):
            neg_exp = jnp.exp(scores[h, r : r + 64] - highest)
            total = total + jnp.sum(neg_exp.reshape(8, 8, CHUNK), 0)
            scores[h, r : r + 64] = neg_exp
        pos_exp = jnp.exp(pos_score - highest)
        total = pos_exp + jnp.sum(total, 0, keepdims=True)
        pos_weight = live * (pos_exp / total - 1.0)
        scale = live / total
        for r in range(0, NEG, 64):
            weights[r : r + 64, lanes] = (scores[h, r : r + 64] * scale).astype(BF)
        grad[h] = dot(neg_t[...], weights[:, lanes])
        one, two = twice(jnp.bitwise_and(keys_ref[1:2, part * PER : (part + 1) * PER], LOCAL - 1))
        k, m = place_ref[2 * part], place_ref[2 * part + 1]
        back_ref[k, SEND:BACK, :] = labels(asked[:, 0:PER], one)
        back_ref[m, SEND:BACK, :] = labels(asked[:, PER:], two)
        for r in range(0, D, 80):
            pos_grad = (pos_weight * q_ref[r : r + 80, own].astype(F32)).astype(BF)
            back_ref[k, r : r + 80, :] = pos_grad[:, 0:PER]
            back_ref[m, r : r + 80, :] = pos_grad[:, PER:]
        if part == 0:
            loads[1].wait()
            loads[2].wait()
        for r in range(0, HALF, 48):
            n, e = min(48, HALF - r), min(48, SECOND - r)
            ga = grad[h, r : r + n] + pos_weight * pos[h, r : r + n]
            gb = grad[h, HALF + r : HALF + r + n] + pos_weight * pos[h, HALF + r : HALF + r + n]
            if e > n:
                none = jnp.zeros((e - n, CHUNK), F32)
                ga, gb = jnp.concatenate([ga, none], 0), jnp.concatenate([gb, none], 0)
            for factor, out in ((w_ref, lhs_g), (l_ref, rel_g)):
                fa = factor[r : r + e, own].astype(F32)
                fb = factor[SECOND + r : SECOND + r + e, own].astype(F32)
                out[r : r + e, own] = (ga * fa + gb * fb).astype(BF)
                out[SECOND + r : SECOND + r + e, own] = (gb * fa - ga * fb).astype(BF)

    stores = [move(back_ref.at[:, 0:D], back_hbm.at[:, 0:D])]
    wide = 4 * PER
    for c in range(0, EDGES, wide):
        packed = keys_ref[0:1, c : c + wide]
        marks = onehot(rel_of(packed), RELP)
        for t in range(0, RELP, 2 * PER):
            part = dot_t(rel_g[:, c : c + wide], marks[t : t + 2 * PER])
            lanes = slice(t, t + 2 * PER)
            total_rel[:, lanes] = part if c == 0 else total_rel[:, lanes] + part
    own = pl.multiple_of(lax.axis_index("core") * (RELP // 2), RELP // 2)
    other = pl.multiple_of((1 - lax.axis_index("core")) * (RELP // 2), RELP // 2)
    for ref, start, hbm in ((other_ref, other, other_hbm), (own_ref, own, own_hbm)):
        for at in range(4):
            lanes = pl.ds(start + at * PER, PER)
            both = jnp.concatenate([total_rel[0:HALF, lanes], total_rel[SECOND : SECOND + HALF, lanes]], 0)
            ref[at, 0:D, :] = both.astype(BF)
            ref[at, D:TALL, :] = jnp.zeros((TALL - D, PER), BF)
        stores.append(move(ref, hbm))
    for c in range(0, EDGES, wide):
        marks = onehot(lhs_of(keys_ref[0:1, c : c + wide]), LOCAL)
        part = dot_t(lhs_g[:, c : c + wide], marks)
        part = jnp.concatenate([part[:HALF], part[SECOND : SECOND + HALF]], 0)
        lhs_ref[...] = part if c == 0 else lhs_ref[...] + part
    for c in range(0, STEPS, 2):
        part = dot_t(q_ref[...], weights[c * PER : (c + 2) * PER, :])
        for h in (0, 1):
            both = part[:, h * PER : (h + 1) * PER]
            top = both[0:FOLD]
            low = jnp.concatenate([both[FOLD:D], jnp.zeros((2 * FOLD - D, PER), F32)], 0)
            first = lax.broadcasted_iota(jnp.int32, top.shape, 1) < 64
            k, m = place_ref[2 * (c + h)], place_ref[2 * (c + h) + 1]
            back_ref[k, D:SEND, :] = jnp.where(first, top, pltpu.roll(low, 64, 1)).astype(BF)
            back_ref[m, D:SEND, :] = jnp.where(first, pltpu.roll(top, 64, 1), low).astype(BF)
    stores.append(move(back_ref.at[:, D:BACK], back_hbm.at[:, D:BACK]))
    for copy in stores:
        copy.wait()


BUFFERS = 4
COPIES = 2 * OWNERS + 7


def edges(place, keys, halves, query, left, weight):
    anywhere = pl.BlockSpec(memory_space=pl.ANY)
    return pl.pallas_call(
        edge_kernel,
        in_specs=[pl.BlockSpec(memory_space=pltpu.SMEM), pl.BlockSpec(memory_space=pltpu.VMEM)] + [anywhere] * 11,
        out_specs=[anywhere] * 3 + [pl.BlockSpec(memory_space=pltpu.VMEM)],
        out_shape=[
            jax.ShapeDtypeStruct((OWNERS, BACK, PER), BF),
            jax.ShapeDtypeStruct((4, TALL, PER), BF),
            jax.ShapeDtypeStruct((4, TALL, PER), BF),
            jax.ShapeDtypeStruct((D, LOCAL), F32),
        ],
        scratch_shapes=[
            pltpu.VMEM((OWNERS, D, LOCAL), BF),
            pltpu.VMEM((D, NEG), BF),
            pltpu.VMEM((NEG, D), BF),
            pltpu.VMEM((NEG, EDGES), BF),
            pltpu.VMEM((D, EDGES), BF),
            pltpu.VMEM((TALL, EDGES), BF),
            pltpu.VMEM((TALL, EDGES), BF),
            pltpu.VMEM((OWNERS, BACK, PER), BF),
            pltpu.VMEM((TALL, EDGES), BF),
            pltpu.VMEM((TALL, EDGES), BF),
            pltpu.VMEM((BUFFERS, NEG, CHUNK), F32),
            pltpu.VMEM((BUFFERS, D, CHUNK), F32),
            pltpu.VMEM((BUFFERS, D, CHUNK), F32),
            pltpu.VMEM((TALL, RELP), F32),
            pltpu.VMEM((4, TALL, PER), BF),
            pltpu.VMEM((4, TALL, PER), BF),
            pltpu.SemaphoreType.DMA((COPIES,)),
        ],
        compiler_params=pltpu.CompilerParams(vmem_limit_bytes=58 * MIB),
        cost_estimate=pl.CostEstimate(flops=8_000_000_000, bytes_accessed=20_000_000, transcendentals=2_100_000),
        name="edges",
    )(place, keys, *halves, query, left, weight)


def spread_kernel(axis, *refs):
    ins, outs = refs[:-4], refs[-4:]
    n = outs[0].shape[0]
    for d in range(4):
        rows = pl.ds(jnp.bitwise_and(lax.axis_index(axis) + d, 3) * n, n)
        total = ins[0][rows].astype(F32)
        for ref in ins[1:]:
            total = total + ref[rows].astype(F32)
        outs[d][...] = total.astype(BF)


def spread(axis, parts):
    n = parts[0].shape[0]
    return pl.pallas_call(
        functools.partial(spread_kernel, axis),
        out_shape=[jax.ShapeDtypeStruct((n // 4, TALL, PER), BF)] * 4,
        name="spread",
    )(*parts)


def add_four(parts):
    own, one, two, three = (part.astype(F32) for part in parts)
    return ((own + two) + (one + three)).astype(BF)


def adagrad(table, accum, grad):
    new_accum = accum + jnp.mean(grad * grad, 0, keepdims=True)
    return table - grad * (LEARN / (jnp.sqrt(new_accum) + TINY)), new_accum


def right_kernel(partner_ref, ext_ref, back_ref, new_ref, accum_ref, pos, neg, m_pos, m_one, m_two):
    del partner_ref
    for s in range(OWNERS):
        lanes = slice(s * PER, (s + 1) * PER)
        pos[:, lanes] = back_ref[s, 0:D, :]
        neg[:, lanes] = back_ref[s, D:SEND, :]
        named = back_ref[s, SEND:BACK, :].astype(F32).astype(jnp.int32)
        m_pos[:, lanes] = onehot(named[0:1], LOCAL)
        m_one[:, lanes], m_two[:, lanes] = fold_marks(onehot(named[1:2], LOCAL))
    low = dot_t(neg[...], m_two[...])[0 : D - FOLD]
    grad = dot_t(pos[...], m_pos[...]) + jnp.concatenate([dot_t(neg[...], m_one[...]), low], 0)
    new_ref[...], accum_ref[...] = adagrad(ext_ref[0, 0:D, :], ext_ref[0, D : D + 1, :], grad)


def right_update(partner, ext_all, back):
    whole = lambda shape: pl.BlockSpec(shape, lambda i, p: (0,) * len(shape))
    marks = pltpu.VMEM((LOCAL, OWNERS * PER), BF)
    return pl.pallas_call(
        right_kernel,
        grid_spec=pltpu.PrefetchScalarGridSpec(
            num_scalar_prefetch=1,
            grid=(1,),
            in_specs=[
                pl.BlockSpec((1, D + 8, LOCAL), lambda i, p: (p[0], 0, 0)),
                whole((OWNERS, BACK, PER)),
            ],
            out_specs=[whole((D, LOCAL)), whole((1, LOCAL))],
            scratch_shapes=[
                pltpu.VMEM((D, OWNERS * PER), BF),
                pltpu.VMEM((FOLD, OWNERS * PER), BF),
                marks,
                marks,
                marks,
            ],
        ),
        out_shape=[jax.ShapeDtypeStruct((D, LOCAL), F32), jax.ShapeDtypeStruct((1, LOCAL), F32)],
        compiler_params=pltpu.CompilerParams(vmem_limit_bytes=58 * MIB),
        cost_estimate=pl.CostEstimate(flops=2_000_000_000, bytes_accessed=5_000_000, transcendentals=0),
        name="right_update",
    )(partner, ext_all, back)


def left_kernel(table_ref, accum_ref, grad_ref, new_ref, new_accum_ref):
    new_ref[...], new_accum_ref[...] = adagrad(table_ref[...], accum_ref[...], grad_ref[...])


def left_update(table, accum, grad):
    return pl.pallas_call(
        left_kernel,
        out_shape=[jax.ShapeDtypeStruct((D, LOCAL), F32), jax.ShapeDtypeStruct((1, LOCAL), F32)],
        name="left_update",
    )(table, accum, grad)


def relation_kernel(table_ref, accum_ref, own_ref, other_ref, new_ref, new_accum_ref):
    for t in range(RELP // PER):
        owned = lax.axis_index("core") == t // 4
        back = jnp.bitwise_and(lax.axis_index("x") - t, 3)
        lanes = slice(t * PER, min((t + 1) * PER, REL))
        grad = jnp.where(owned, own_ref[back, 0:D, :], other_ref[back, 0:D, :]).astype(F32)
        grad = grad[:, : lanes.stop - lanes.start]
        new_ref[:, lanes], new_accum_ref[:, lanes] = adagrad(table_ref[:, lanes], accum_ref[:, lanes], grad)


def relation_update(table, accum, own, other):
    return pl.pallas_call(
        relation_kernel,
        out_shape=[jax.ShapeDtypeStruct((D, REL), F32), jax.ShapeDtypeStruct((1, REL), F32)],
        compiler_params=pltpu.CompilerParams(vmem_limit_bytes=58 * MIB),
        name="relation_update",
    )(table, accum, own, other)


CORES = [(0, 1), (1, 0)]
GRP, ROW, CHIPS = ("x", "core"), ("z", "y"), ("x", "z", "y")


def shift(value, axis, distance):
    return lax.ppermute(value, axis, [(i, (i + distance) & 3) for i in range(4)])


def other_core(value):
    return lax.ppermute(value, "core", CORES)


def pick(near, target, group):
    back = ((group >> 1) - (target >> 1)) & 3
    return jnp.where(back < 2, jnp.where(back == 0, near[0], near[1]), jnp.where(back == 2, near[2], near[3]))


def relative(owner, z, y):
    return (((z - (owner >> 2)) & 3) << 2) | ((y - (owner & 3)) & 3)


def gather_rows(first, second):
    lines = [[first] + [shift(first, "y", d) for d in (2, 1, 3)], [second] + [shift(second, "z", d) for d in (2, 1, 3)]]
    (f0, f2, f1, f3), (s0, s2, s1, s3) = lax.optimization_barrier(lines)
    first, second = jnp.stack([f0, f1, f2, f3]), jnp.stack([s0, s1, s2, s3])
    f2, s2 = shift(first, "z", 2), shift(second, "y", 2)
    f1, s1 = shift(first, "z", 1), shift(second, "y", 1)
    f3, s3 = shift(first, "z", 3), shift(second, "y", 3)
    return [first, f1, f2, f3, second, s1, s2, s3]


def body(
    lhs_emb,
    lhs_accum,
    rhs_emb,
    rhs_accum,
    rel_emb,
    rel_accum,
    partner,
    edge_lhs,
    edge_rhs,
    edge_rel,
    edge_count,
    neg_rhs,
):
    lhs_t, rhs_t, rel_t = lhs_emb[0].T, rhs_emb[0].T, rel_emb.T
    x, core, z, y = (lax.axis_index(axis) for axis in ("x", "core", "z", "y"))
    group = 2 * x + core

    mine = rhs_t.astype(BF)
    target = partner[0]
    other = other_core(partner)[0]
    near = [mine] + [shift(mine, "x", d) for d in (1, 2, 3)]
    here = pick(near, target, group)
    across = other_core(pick(near, other, group))
    held = jnp.where((target & 1) == (group & 1), here, across)
    order = jnp.arange(OWNERS, dtype=jnp.int32)
    place = relative(order, z, y)
    live = (jnp.arange(EDGES, dtype=jnp.int32) < edge_count[0, 0]).astype(jnp.int32)
    pos_key = (relative(edge_rhs[0, 0] >> 8, z, y) << 27) | ((edge_rhs[0, 0] & (LOCAL - 1)) << 19)
    pos_key = pos_key | (edge_rel[0, 0] << 9) | (edge_lhs[0, 0] << 1) | live
    neg_key = (relative(neg_rhs[0, 0] >> 8, z, y) << 8) | (neg_rhs[0, 0] & (LOCAL - 1))
    spare = jnp.full((EDGES - NEG,), 1 << 30, jnp.int32)
    keys = jnp.stack([pos_key, jnp.concatenate([neg_key, spare])])
    exact = jnp.concatenate([rhs_t, jnp.broadcast_to(rhs_accum, (8, LOCAL))], 0)
    exact, held, keys, place = lax.optimization_barrier((exact, held, keys, place))
    ext_all = lax.all_gather(exact, GRP, axis=0, tiled=False)
    halves = gather_rows(held[:, :PER], held[:, PER:])
    keys = lax.sort(keys, is_stable=False)
    left, weight, query = make_query(keys, lhs_t, rel_t)

    back, own, other, lhs_sum = edges(place, keys, halves, query, left, weight)
    returned = lax.all_to_all(back, ROW, 0, 0, tiled=True)
    new_lhs, new_lhs_accum = left_update(lhs_t, lhs_accum, lhs_sum)
    new_rhs, new_rhs_accum = right_update(partner, ext_all, returned)
    pieces = spread("x", [own, other_core(other)])
    total = add_four([pieces[0]] + [shift(pieces[d], "x", d) for d in (1, 2, 3)])
    total = add_four([total] + [shift(total, "z", d) for d in (1, 2, 3)])
    pieces = [total] + [shift(total, "y", d) for d in (1, 2, 3)]
    pieces, new_lhs, new_rhs = lax.optimization_barrier((pieces, new_lhs, new_rhs))
    total = add_four(pieces)
    pieces = [total] + [shift(total, "x", d) for d in (1, 2, 3)]
    own = jnp.stack(pieces).reshape(4, TALL, PER)
    new_rel, new_rel_accum = relation_update(rel_t, rel_accum[None], own, other_core(own))
    return (
        new_lhs.T[None],
        new_lhs_accum,
        new_rhs.T[None],
        new_rhs_accum,
        new_rel.T,
        new_rel_accum[0],
    )


def solution(mesh):
    fine = jax.sharding.Mesh(mesh.devices.reshape(4, 2, 4, 4), ("x", "core", "z", "y"))
    rows = P(GRP, ROW, None)
    in_specs = (rows, P(GRP, ROW), rows, P(GRP, ROW), P(), P(), P(GRP), rows, rows, rows, P(GRP, ROW), rows)
    out_specs = (rows, P(GRP, ROW), rows, P(GRP, ROW), P(), P())
    return jax.shard_map(body, mesh=fine, in_specs=in_specs, out_specs=out_specs, check_vma=False)
```

```python
import functools

import jax
import jax.numpy as jnp
from jax import lax
from jax.experimental import pallas as pl
from jax.experimental.pallas import tpu as pltpu
from jax.sharding import PartitionSpec as P

LEARN = 0.25
TINY = 1e-10
BF = jnp.bfloat16
F32 = jnp.float32
D = 400
HALF = 200
SECOND = 208
TALL = 2 * SECOND
REL = 1000
RELP = 1024
LOCAL = 256
EDGES = 2048
NEG = 1024
OWNERS = 16
PER = 128
FOLD = 208
SEND = D + FOLD
BACK = SEND + 16
CHUNK = 256
STEPS = EDGES // CHUNK
MIB = 1024 * 1024


def onehot(index, count):
    rows = lax.broadcasted_iota(jnp.int32, (count, index.shape[1]), 0)
    return jnp.where(rows == index, 1.0, 0.0).astype(BF)


def dot(a, b):
    return jnp.dot(a, b, preferred_element_type=F32)


def dot_t(a, b):
    return lax.dot_general(a, b, (((1,), (1,)), ((), ())), preferred_element_type=F32)


def split(value):
    high = value.astype(BF)
    return high, (value - high.astype(F32)).astype(BF)


def lhs_of(packed):
    return jnp.bitwise_and(jnp.right_shift(packed, 1), LOCAL - 1)


def rel_of(packed):
    return jnp.bitwise_and(jnp.right_shift(packed, 9), RELP - 1)


def query_kernel(keys_ref, lhs_ref, rel_ref, l_ref, w_ref, q_ref, lhs_two, rel_two):
    @pl.when(pl.program_id(0) == 0)
    def _():
        high, low = split(lhs_ref[...])
        lhs_two[0:D, :] = high
        lhs_two[D : 2 * D, :] = low
        rel_two[...] = jnp.zeros_like(rel_two)
        high, low = split(rel_ref[...])
        rel_two[0:D, 0:REL] = high
        rel_two[D : 2 * D, 0:REL] = low

    packed = keys_ref[0:1, :]
    both = dot(lhs_two[...], onehot(lhs_of(packed), LOCAL))
    left = both[0:D] + both[D : 2 * D]
    both = dot(rel_two[...], onehot(rel_of(packed), RELP))
    weight = both[0:D] + both[D : 2 * D]
    none = jnp.zeros((SECOND - HALF, CHUNK), F32)
    l_ref[...] = jnp.concatenate([left[:HALF], none, left[HALF:], none], 0).astype(BF)
    w_ref[...] = jnp.concatenate([weight[:HALF], none, weight[HALF:], none], 0).astype(BF)
    la, lb, wa, wb = left[:HALF], left[HALF:], weight[:HALF], weight[HALF:]
    q_ref[...] = jnp.concatenate([la * wa - lb * wb, la * wb + lb * wa], 0).astype(BF)


def make_query(keys, lhs_t, rel_t):
    wide = pl.BlockSpec((D, CHUNK), lambda i: (0, i))
    tall = pl.BlockSpec((TALL, CHUNK), lambda i: (0, i))
    return pl.pallas_call(
        query_kernel,
        grid=(STEPS,),
        in_specs=[
            pl.BlockSpec((2, CHUNK), lambda i: (0, i)),
            pl.BlockSpec((D, LOCAL), lambda i: (0, 0)),
            pl.BlockSpec((D, REL), lambda i: (0, 0)),
        ],
        out_specs=[tall, tall, wide],
        out_shape=[
            jax.ShapeDtypeStruct((TALL, EDGES), BF),
            jax.ShapeDtypeStruct((TALL, EDGES), BF),
            jax.ShapeDtypeStruct((D, EDGES), BF),
        ],
        scratch_shapes=[pltpu.VMEM((2 * D, LOCAL), BF), pltpu.VMEM((2 * D, RELP), BF)],
        compiler_params=pltpu.CompilerParams(vmem_limit_bytes=58 * MIB),
        cost_estimate=pl.CostEstimate(flops=5_000_000_000, bytes_accessed=10_000_000, transcendentals=0),
        name="make_query",
    )(keys, lhs_t, rel_t)


def fold_marks(marks):
    first = lax.broadcasted_iota(jnp.int32, marks.shape, 1) < 64
    none = jnp.zeros_like(marks)
    return jnp.where(first, marks, none), jnp.where(first, none, marks)


def twice(row):
    first = lax.broadcasted_iota(jnp.int32, row.shape, 1) < 64
    turned = pltpu.roll(row, 64, 1)
    return jnp.where(first, row, turned), jnp.where(first, turned, row)


def labels(pos, neg):
    row = lax.broadcasted_iota(jnp.int32, (16, PER), 0)
    return jnp.where(row == 0, pos, jnp.where(row == 1, neg, 0)).astype(F32).astype(BF)


def edge_kernel(
    place_ref, keys_ref, a0, a1, a2, a3, b0, b1, b2, b3, q_hbm, l_hbm, w_hbm, back_hbm, own_hbm, other_hbm, lhs_ref,
    table, neg_t, neg_n, weights, q_ref, l_ref, w_ref, back_ref, lhs_g, rel_g, scores, pos, grad, total_rel, own_ref, other_ref, sems,
):
    count = iter(range(COPIES))

    def move(source, target):
        copy = pltpu.make_async_copy(source, target, sems.at[next(count)])
        copy.start()
        return copy

    blocks, loads = [], []
    for z, a in enumerate((a0, a1, a2, a3)):
        for y, b in enumerate((b0, b1, b2, b3)):
            at = 4 * z + y
            blocks.append((move(a.at[y], table.at[at, :, 0:PER]), move(b.at[z], table.at[at, :, PER:LOCAL])))
    for hbm, ref in ((q_hbm, q_ref), (l_hbm, l_ref), (w_hbm, w_ref)):
        loads.append(move(hbm, ref))
    for pair in blocks:
        for copy in pair:
            copy.wait()

    for c in range(STEPS):
        here = jnp.bitwise_and(keys_ref[1:2, c * PER : (c + 1) * PER], LOCAL - 1)
        one, two = fold_marks(onehot(here, LOCAL))
        rows = dot(table[2 * c], one) + dot(table[2 * c + 1], two)
        lanes = slice(c * PER, (c + 1) * PER)
        neg_t[:, lanes] = rows.astype(BF)
        neg_n[lanes, :] = rows.T.astype(BF)

    loads[0].wait()
    for part in range(STEPS):
        h = part % BUFFERS
        lanes = own = slice(part * CHUNK, (part + 1) * CHUNK)
        packed = keys_ref[0:1, lanes]
        live = jnp.bitwise_and(packed, 1).astype(F32)
        query = q_ref[:, own]
        asked = jnp.bitwise_and(jnp.right_shift(packed, 19), LOCAL - 1)
        marks = onehot(asked, LOCAL)
        scores[h] = dot(neg_n[...], query)
        pos[h, :, 0:PER] = dot(table[2 * part], marks[:, 0:PER])
        pos[h, :, PER:] = dot(table[2 * part + 1], marks[:, PER:])
        pos_score = jnp.zeros((8, CHUNK), F32)
        for r in range(0, D, 80):
            product = q_ref[r : r + 80, own].astype(F32) * pos[h, r : r + 80]
            pos_score = pos_score + jnp.sum(product.reshape(10, 8, CHUNK), 0)
        pos_score = jnp.sum(pos_score, 0, keepdims=True)
        highest = jnp.broadcast_to(pos_score, (8, CHUNK))
        for r in range(0, NEG, 64):
            highest = jnp.maximum(highest, jnp.max(scores[h, r : r + 64].reshape(8, 8, CHUNK), 0))
        highest = jnp.max(highest, 0, keepdims=True)
        total = jnp.zeros((8, CHUNK), F32)
        for r in range(0, NEG, 64):
            neg_exp = jnp.exp(scores[h, r : r + 64] - highest)
            total = total + jnp.sum(neg_exp.reshape(8, 8, CHUNK), 0)
            scores[h, r : r + 64] = neg_exp
        pos_exp = jnp.exp(pos_score - highest)
        total = pos_exp + jnp.sum(total, 0, keepdims=True)
        pos_weight = live * (pos_exp / total - 1.0)
        scale = live / total
        for r in range(0, NEG, 64):
            weights[r : r + 64, lanes] = (scores[h, r : r + 64] * scale).astype(BF)
        grad[h] = dot(neg_t[...], weights[:, lanes])
        one, two = twice(jnp.bitwise_and(keys_ref[1:2, part * PER : (part + 1) * PER], LOCAL - 1))
        k, m = place_ref[2 * part], place_ref[2 * part + 1]
        back_ref[k, SEND:BACK, :] = labels(asked[:, 0:PER], one)
        back_ref[m, SEND:BACK, :] = labels(asked[:, PER:], two)
        for r in range(0, D, 80):
            pos_grad = (pos_weight * q_ref[r : r + 80, own].astype(F32)).astype(BF)
            back_ref[k, r : r + 80, :] = pos_grad[:, 0:PER]
            back_ref[m, r : r + 80, :] = pos_grad[:, PER:]
        if part == 0:
            loads[1].wait()
            loads[2].wait()
        for r in range(0, HALF, 48):
            n, e = min(48, HALF - r), min(48, SECOND - r)
            ga = grad[h, r : r + n] + pos_weight * pos[h, r : r + n]
            gb = grad[h, HALF + r : HALF + r + n] + pos_weight * pos[h, HALF + r : HALF + r + n]
            if e > n:
                none = jnp.zeros((e - n, CHUNK), F32)
                ga, gb = jnp.concatenate([ga, none], 0), jnp.concatenate([gb, none], 0)
            for factor, out in ((w_ref, lhs_g), (l_ref, rel_g)):
                fa = factor[r : r + e, own].astype(F32)
                fb = factor[SECOND + r : SECOND + r + e, own].astype(F32)
                out[r : r + e, own] = (ga * fa + gb * fb).astype(BF)
                out[SECOND + r : SECOND + r + e, own] = (gb * fa - ga * fb).astype(BF)

    stores = [move(back_ref.at[:, 0:D], back_hbm.at[:, 0:D])]
    wide = 4 * PER
    for c in range(0, EDGES, wide):
        packed = keys_ref[0:1, c : c + wide]
        marks = onehot(rel_of(packed), RELP)
        for t in range(0, RELP, 2 * PER):
            part = dot_t(rel_g[:, c : c + wide], marks[t : t + 2 * PER])
            lanes = slice(t, t + 2 * PER)
            total_rel[:, lanes] = part if c == 0 else total_rel[:, lanes] + part
    own = pl.multiple_of(lax.axis_index("core") * (RELP // 2), RELP // 2)
    other = pl.multiple_of((1 - lax.axis_index("core")) * (RELP // 2), RELP // 2)
    for ref, start, hbm in ((other_ref, other, other_hbm), (own_ref, own, own_hbm)):
        for at in range(4):
            lanes = pl.ds(start + at * PER, PER)
            both = jnp.concatenate([total_rel[0:HALF, lanes], total_rel[SECOND : SECOND + HALF, lanes]], 0)
            ref[at, 0:D, :] = both.astype(BF)
            ref[at, D:TALL, :] = jnp.zeros((TALL - D, PER), BF)
        stores.append(move(ref, hbm))
    for c in range(0, EDGES, wide):
        marks = onehot(lhs_of(keys_ref[0:1, c : c + wide]), LOCAL)
        part = dot_t(lhs_g[:, c : c + wide], marks)
        part = jnp.concatenate([part[:HALF], part[SECOND : SECOND + HALF]], 0)
        lhs_ref[...] = part if c == 0 else lhs_ref[...] + part
    for c in range(0, STEPS, 2):
        part = dot_t(q_ref[...], weights[c * PER : (c + 2) * PER, :])
        for h in (0, 1):
            both = part[:, h * PER : (h + 1) * PER]
            top = both[0:FOLD]
            low = jnp.concatenate([both[FOLD:D], jnp.zeros((2 * FOLD - D, PER), F32)], 0)
            first = lax.broadcasted_iota(jnp.int32, top.shape, 1) < 64
            k, m = place_ref[2 * (c + h)], place_ref[2 * (c + h) + 1]
            back_ref[k, D:SEND, :] = jnp.where(first, top, pltpu.roll(low, 64, 1)).astype(BF)
            back_ref[m, D:SEND, :] = jnp.where(first, pltpu.roll(top, 64, 1), low).astype(BF)
    stores.append(move(back_ref.at[:, D:BACK], back_hbm.at[:, D:BACK]))
    for copy in stores:
        copy.wait()


BUFFERS = 4
COPIES = 2 * OWNERS + 7


def edges(place, keys, halves, query, left, weight):
    anywhere = pl.BlockSpec(memory_space=pl.ANY)
    return pl.pallas_call(
        edge_kernel,
        in_specs=[pl.BlockSpec(memory_space=pltpu.SMEM), pl.BlockSpec(memory_space=pltpu.VMEM)] + [anywhere] * 11,
        out_specs=[anywhere] * 3 + [pl.BlockSpec(memory_space=pltpu.VMEM)],
        out_shape=[
            jax.ShapeDtypeStruct((OWNERS, BACK, PER), BF),
            jax.ShapeDtypeStruct((4, TALL, PER), BF),
            jax.ShapeDtypeStruct((4, TALL, PER), BF),
            jax.ShapeDtypeStruct((D, LOCAL), F32),
        ],
        scratch_shapes=[
            pltpu.VMEM((OWNERS, D, LOCAL), BF),
            pltpu.VMEM((D, NEG), BF),
            pltpu.VMEM((NEG, D), BF),
            pltpu.VMEM((NEG, EDGES), BF),
            pltpu.VMEM((D, EDGES), BF),
            pltpu.VMEM((TALL, EDGES), BF),
            pltpu.VMEM((TALL, EDGES), BF),
            pltpu.VMEM((OWNERS, BACK, PER), BF),
            pltpu.VMEM((TALL, EDGES), BF),
            pltpu.VMEM((TALL, EDGES), BF),
            pltpu.VMEM((BUFFERS, NEG, CHUNK), F32),
            pltpu.VMEM((BUFFERS, D, CHUNK), F32),
            pltpu.VMEM((BUFFERS, D, CHUNK), F32),
            pltpu.VMEM((TALL, RELP), F32),
            pltpu.VMEM((4, TALL, PER), BF),
            pltpu.VMEM((4, TALL, PER), BF),
            pltpu.SemaphoreType.DMA((COPIES,)),
        ],
        compiler_params=pltpu.CompilerParams(vmem_limit_bytes=58 * MIB),
        cost_estimate=pl.CostEstimate(flops=8_000_000_000, bytes_accessed=20_000_000, transcendentals=2_100_000),
        name="edges",
    )(place, keys, *halves, query, left, weight)


def spread_kernel(axis, *refs):
    ins, outs = refs[:-4], refs[-4:]
    n = outs[0].shape[0]
    for d in range(4):
        rows = pl.ds(jnp.bitwise_and(lax.axis_index(axis) + d, 3) * n, n)
        total = ins[0][rows].astype(F32)
        for ref in ins[1:]:
            total = total + ref[rows].astype(F32)
        outs[d][...] = total.astype(BF)


def spread(axis, parts):
    n = parts[0].shape[0]
    return pl.pallas_call(
        functools.partial(spread_kernel, axis),
        out_shape=[jax.ShapeDtypeStruct((n // 4, TALL, PER), BF)] * 4,
        name="spread",
    )(*parts)


def add_four(parts):
    own, one, two, three = (part.astype(F32) for part in parts)
    return ((own + two) + (one + three)).astype(BF)


def adagrad(table, accum, grad):
    new_accum = accum + jnp.mean(grad * grad, 0, keepdims=True)
    return table - grad * (LEARN / (jnp.sqrt(new_accum) + TINY)), new_accum


def right_kernel(partner_ref, ext_ref, back_ref, new_ref, accum_ref, pos, neg, m_pos, m_one, m_two):
    del partner_ref
    for s in range(OWNERS):
        lanes = slice(s * PER, (s + 1) * PER)
        pos[:, lanes] = back_ref[s, 0:D, :]
        neg[:, lanes] = back_ref[s, D:SEND, :]
        named = back_ref[s, SEND:BACK, :].astype(F32).astype(jnp.int32)
        m_pos[:, lanes] = onehot(named[0:1], LOCAL)
        m_one[:, lanes], m_two[:, lanes] = fold_marks(onehot(named[1:2], LOCAL))
    low = dot_t(neg[...], m_two[...])[0 : D - FOLD]
    grad = dot_t(pos[...], m_pos[...]) + jnp.concatenate([dot_t(neg[...], m_one[...]), low], 0)
    new_ref[...], accum_ref[...] = adagrad(ext_ref[0, 0:D, :], ext_ref[0, D : D + 1, :], grad)


def right_update(partner, ext_all, back):
    whole = lambda shape: pl.BlockSpec(shape, lambda i, p: (0,) * len(shape))
    marks = pltpu.VMEM((LOCAL, OWNERS * PER), BF)
    return pl.pallas_call(
        right_kernel,
        grid_spec=pltpu.PrefetchScalarGridSpec(
            num_scalar_prefetch=1,
            grid=(1,),
            in_specs=[
                pl.BlockSpec((1, D + 8, LOCAL), lambda i, p: (p[0], 0, 0)),
                whole((OWNERS, BACK, PER)),
            ],
            out_specs=[whole((D, LOCAL)), whole((1, LOCAL))],
            scratch_shapes=[
                pltpu.VMEM((D, OWNERS * PER), BF),
                pltpu.VMEM((FOLD, OWNERS * PER), BF),
                marks,
                marks,
                marks,
            ],
        ),
        out_shape=[jax.ShapeDtypeStruct((D, LOCAL), F32), jax.ShapeDtypeStruct((1, LOCAL), F32)],
        compiler_params=pltpu.CompilerParams(vmem_limit_bytes=20 * MIB),
        cost_estimate=pl.CostEstimate(flops=2_000_000_000, bytes_accessed=5_000_000, transcendentals=0),
        name="right_update",
    )(partner, ext_all, back)


def left_kernel(table_ref, accum_ref, grad_ref, new_ref, new_accum_ref):
    new_ref[...], new_accum_ref[...] = adagrad(table_ref[...], accum_ref[...], grad_ref[...])


def left_update(table, accum, grad):
    return pl.pallas_call(
        left_kernel,
        out_shape=[jax.ShapeDtypeStruct((D, LOCAL), F32), jax.ShapeDtypeStruct((1, LOCAL), F32)],
        name="left_update",
    )(table, accum, grad)


def relation_kernel(table_ref, accum_ref, own_ref, other_ref, new_ref, new_accum_ref):
    for t in range(RELP // PER):
        owned = lax.axis_index("core") == t // 4
        back = jnp.bitwise_and(lax.axis_index("x") - t, 3)
        lanes = slice(t * PER, min((t + 1) * PER, REL))
        grad = jnp.where(owned, own_ref[back, 0:D, :], other_ref[back, 0:D, :]).astype(F32)
        grad = grad[:, : lanes.stop - lanes.start]
        new_ref[:, lanes], new_accum_ref[:, lanes] = adagrad(table_ref[:, lanes], accum_ref[:, lanes], grad)


def relation_update(table, accum, own, other):
    return pl.pallas_call(
        relation_kernel,
        out_shape=[jax.ShapeDtypeStruct((D, REL), F32), jax.ShapeDtypeStruct((1, REL), F32)],
        compiler_params=pltpu.CompilerParams(vmem_limit_bytes=58 * MIB),
        name="relation_update",
    )(table, accum, own, other)


CORES = [(0, 1), (1, 0)]
GRP, ROW, CHIPS = ("x", "core"), ("z", "y"), ("x", "z", "y")


def shift(value, axis, distance):
    return lax.ppermute(value, axis, [(i, (i + distance) & 3) for i in range(4)])


def other_core(value):
    return lax.ppermute(value, "core", CORES)


def pick(near, target, group):
    back = ((group >> 1) - (target >> 1)) & 3
    return jnp.where(back < 2, jnp.where(back == 0, near[0], near[1]), jnp.where(back == 2, near[2], near[3]))


def relative(owner, z, y):
    return (((z - (owner >> 2)) & 3) << 2) | ((y - (owner & 3)) & 3)


def gather_rows(first, second):
    lines = [[first] + [shift(first, "y", d) for d in (2, 1, 3)], [second] + [shift(second, "z", d) for d in (2, 1, 3)]]
    (f0, f2, f1, f3), (s0, s2, s1, s3) = lax.optimization_barrier(lines)
    first, second = jnp.stack([f0, f1, f2, f3]), jnp.stack([s0, s1, s2, s3])
    f2, s2 = shift(first, "z", 2), shift(second, "y", 2)
    f1, s1 = shift(first, "z", 1), shift(second, "y", 1)
    f3, s3 = shift(first, "z", 3), shift(second, "y", 3)
    return [first, f1, f2, f3, second, s1, s2, s3]


def body(
    lhs_emb,
    lhs_accum,
    rhs_emb,
    rhs_accum,
    rel_emb,
    rel_accum,
    partner,
    edge_lhs,
    edge_rhs,
    edge_rel,
    edge_count,
    neg_rhs,
):
    lhs_t, rhs_t, rel_t = lhs_emb[0].T, rhs_emb[0].T, rel_emb.T
    x, core, z, y = (lax.axis_index(axis) for axis in ("x", "core", "z", "y"))
    group = 2 * x + core

    mine = rhs_t.astype(BF)
    target = partner[0]
    other = other_core(partner)[0]
    near = [mine] + [shift(mine, "x", d) for d in (1, 2, 3)]
    here = pick(near, target, group)
    across = other_core(pick(near, other, group))
    held = jnp.where((target & 1) == (group & 1), here, across)
    order = jnp.arange(OWNERS, dtype=jnp.int32)
    place = relative(order, z, y)
    live = (jnp.arange(EDGES, dtype=jnp.int32) < edge_count[0, 0]).astype(jnp.int32)
    pos_key = (relative(edge_rhs[0, 0] >> 8, z, y) << 27) | ((edge_rhs[0, 0] & (LOCAL - 1)) << 19)
    pos_key = pos_key | (edge_rel[0, 0] << 9) | (edge_lhs[0, 0] << 1) | live
    neg_key = (relative(neg_rhs[0, 0] >> 8, z, y) << 8) | (neg_rhs[0, 0] & (LOCAL - 1))
    spare = jnp.full((EDGES - NEG,), 1 << 30, jnp.int32)
    keys = jnp.stack([pos_key, jnp.concatenate([neg_key, spare])])
    exact = jnp.concatenate([rhs_t, jnp.broadcast_to(rhs_accum, (8, LOCAL))], 0)
    exact, held, keys, place = lax.optimization_barrier((exact, held, keys, place))
    ext_all = lax.all_gather(exact, GRP, axis=0, tiled=False)
    halves = gather_rows(held[:, :PER], held[:, PER:])
    keys = lax.sort(keys, is_stable=False)
    left, weight, query = make_query(keys, lhs_t, rel_t)

    back, own, other, lhs_sum = edges(place, keys, halves, query, left, weight)
    returned = lax.all_to_all(back, ROW, 0, 0, tiled=True)
    new_lhs, new_lhs_accum = left_update(lhs_t, lhs_accum, lhs_sum)
    new_rhs, new_rhs_accum = right_update(partner, ext_all, returned)
    pieces = spread("x", [own, other_core(other)])
    total = add_four([pieces[0]] + [shift(pieces[d], "x", d) for d in (1, 2, 3)])
    total = add_four([total] + [shift(total, "z", d) for d in (1, 2, 3)])
    pieces = [total] + [shift(total, "y", d) for d in (1, 2, 3)]
    pieces, new_lhs, new_rhs = lax.optimization_barrier((pieces, new_lhs, new_rhs))
    total = add_four(pieces)
    pieces = [total] + [shift(total, "x", d) for d in (1, 2, 3)]
    own = jnp.stack(pieces).reshape(4, TALL, PER)
    new_rel, new_rel_accum = relation_update(rel_t, rel_accum[None], own, other_core(own))
    return (
        new_lhs.T[None],
        new_lhs_accum,
        new_rhs.T[None],
        new_rhs_accum,
        new_rel.T,
        new_rel_accum[0],
    )


def solution(mesh):
    fine = jax.sharding.Mesh(mesh.devices.reshape(4, 2, 4, 4), ("x", "core", "z", "y"))
    rows = P(GRP, ROW, None)
    in_specs = (rows, P(GRP, ROW), rows, P(GRP, ROW), P(), P(), P(GRP), rows, rows, rows, P(GRP, ROW), rows)
    out_specs = (rows, P(GRP, ROW), rows, P(GRP, ROW), P(), P())
    return jax.shard_map(body, mesh=fine, in_specs=in_specs, out_specs=out_specs, check_vma=False)
```
